32 devices in a mesh: pipe: 8 (over z, y), tp: 4 (over x, core).
Axes of the slice: x: 2, y: 2, z: 4, core: 2. Of those that a mesh axis runs over, the one named last changes fastest.
Arguments:
- fwd_resid: bfloat16 [8, 512, 4096], P('pipe', 'tp'), may hold values from -6 to 6
- fwd_query: bfloat16 [8, 512, 4096], P('pipe', None, 'tp'), may hold values from -28 to 28
- fwd_keyval: bfloat16 [8, 2, 512, 1024], P('pipe', None, None, 'tp'), may hold values from -8 to 8
- fwd_micro: int32 [8], P('pipe'), may hold values from 0 to 3
- bwd_query: bfloat16 [8, 512, 4096], P('pipe', None, 'tp'), may hold values from -28 to 28
- bwd_keyval: bfloat16 [8, 2, 512, 1024], P('pipe', None, None, 'tp'), may hold values from -8 to 8
- grad_micro: int32 [8], P('pipe'), may hold values from 0 to 3
- grad_in: bfloat16 [8, 512, 4096], P('pipe', 'tp'), may hold values from -6 to 6
- out_weight: bfloat16 [8, 4096, 4096], P('pipe', 'tp'), may hold values from -0.09375 to 0.09375
- doc_starts: int32 [4, 4], replicated, may hold values from 0 to 511, as said below
Outputs:
- fwd_out: bfloat16 [8, 512, 4096], P('pipe', 'tp')
- grad_query: bfloat16 [8, 512, 4096], P('pipe', None, 'tp')
- grad_keyval: bfloat16 [8, 2, 512, 1024], P('pipe', None, None, 'tp')
- grad_weight: bfloat16 [8, 4096, 4096], P('pipe', 'tp')
The draws below stay inside these ranges and needn't reach their ends.
Inputs may be any that keep to these rules, and one draw needn't show every extreme that they name: `doc_starts`: row m holds the first rows of the 4 documents of micro-batch m: it begins with 0 and rises strictly.
All inputs are finite; a program needn't handle non-finite values.
Results may differ from the reference program's by a relative error of at most 0.007.
Values may be sent and summed in bfloat16 or wider, within the bound.
No kernel may reach another device: no remote copies, remote signals or barrier semaphores. Data moves between devices by JAX's collectives and lax.ppermute only.
A program may use at most 128 MiB of HBM per device.

```python
import math
import jax
import jax.numpy as jnp
from jax import lax

R = 512
D = 4096
HEADS = 32
KVH = 8
HD = 128
NDOC = 4
MICRO = 4
PHASES = 8
N_TP = 4


def keys_and_queries(key, which):
    base_key = jax.random.fold_in(key, 7 + which)
    query = jnp.clip(jax.random.normal(jax.random.fold_in(base_key, 1), (PHASES, R, HEADS * HD), jnp.float32), -6.0, 6.0)
    keyval = jnp.clip(jax.random.normal(jax.random.fold_in(base_key, 2), (PHASES, 2, R, KVH * HD), jnp.float32), -6.0, 6.0)
    return (query, keyval)


def draw_fwd_query(key, part):
    return keys_and_queries(key, 0)[0].astype(jnp.bfloat16)


def draw_fwd_keyval(key, part):
    return keys_and_queries(key, 0)[1].astype(jnp.bfloat16)


def draw_bwd_query(key, part):
    return keys_and_queries(key, 1)[0].astype(jnp.bfloat16)


def draw_bwd_keyval(key, part):
    return keys_and_queries(key, 1)[1].astype(jnp.bfloat16)


def draw_doc_starts(key, part):

    def one_row(row_key):
        picked = jax.random.permutation(row_key, R - 1)[:NDOC - 1] + 1
        return jnp.concatenate([jnp.zeros((1,), jnp.int32), jnp.sort(picked).astype(jnp.int32)])
    return jax.vmap(one_row)(jax.random.split(jax.random.fold_in(key, 3), MICRO))


def plant(result, own_key, low, largest):
    spot = [jax.random.randint(jax.random.fold_in(own_key, axis), (), 0, length) for axis, length in enumerate(result.shape)]
    main_axis = result.shape.index(max(result.shape))
    beside = spot[:main_axis] + [(spot[main_axis] + 1) % result.shape[main_axis]] + spot[main_axis + 1:]
    return result.at[tuple(spot)].set(low).at[tuple(beside)].set(largest)


def block_scale(key, extent, pieces, smallest, high):
    level = 1.0
    for dim, blocks in pieces:
        steps = jax.random.uniform(jax.random.fold_in(jax.random.fold_in(key, 6), dim), (blocks,), jnp.float32, smallest / len(pieces), high / len(pieces))
        level = level * jnp.repeat(jnp.exp(steps), extent[dim] // blocks).reshape((-1,) + (1,) * (len(extent) - 1 - dim))
    return level


def gaussian(key, extent, spread, reach, cuts=(), kind=jnp.bfloat16):
    drawn = jax.random.normal(key, extent, jnp.float32) * spread
    if len(cuts) > 0:
        drawn = block_scale(key, extent, cuts, -0.22, 0.18) * drawn
    return jnp.clip(drawn, min=-reach, max=reach).astype(kind)


def setup_inputs(seed: int = 0) -> dict:
    splits = jax.random.split(jax.random.key(seed), 11)
    fwd_resid = gaussian(splits[0], (PHASES, R, D), 1.0, 6.0, ((0, 8), (1, 4)))
    fwd_query = draw_fwd_query(jax.random.fold_in(splits[10], 71), 0)
    fwd_keyval = draw_fwd_keyval(jax.random.fold_in(splits[10], 71), 0)
    fwd_micro = plant(jax.random.randint(splits[3], (PHASES,), 0, MICRO), jax.random.fold_in(splits[3], 1), 0, MICRO - 1).astype(jnp.int32)
    bwd_query = draw_bwd_query(jax.random.fold_in(splits[10], 71), 0)
    bwd_keyval = draw_bwd_keyval(jax.random.fold_in(splits[10], 71), 0)
    grad_micro = plant(jax.random.randint(splits[6], (PHASES,), 0, MICRO), jax.random.fold_in(splits[6], 1), 0, MICRO - 1).astype(jnp.int32)
    grad_in = gaussian(splits[7], (PHASES, R, D), 1.0, 6.0, ((0, 8), (1, 4)))
    out_weight = gaussian(splits[8], (PHASES, HEADS * HD, D), (HEADS * HD) ** -0.5, 0.09375, ((0, 8), (1, 4)))
    doc_starts = draw_doc_starts(jax.random.fold_in(splits[10], 71), 0)
    return dict(fwd_resid=fwd_resid, fwd_query=fwd_query, fwd_keyval=fwd_keyval, fwd_micro=fwd_micro, bwd_query=bwd_query, bwd_keyval=bwd_keyval, grad_micro=grad_micro, grad_in=grad_in, out_weight=out_weight, doc_starts=doc_starts)


def doc_allowed(starts, row_count):
    position = jnp.arange(row_count, dtype=jnp.int32)
    segment = lax.optimization_barrier(jnp.sum((starts[None, :] <= position[:, None]).astype(jnp.int32), axis=1))
    causal = position[None, :] <= position[:, None]
    return causal & (segment[:, None] == segment[None, :])

def pick_starts(start_table, micro_index):
    chosen = jnp.arange(start_table.shape[0], dtype=jnp.int32) == micro_index
    return lax.optimization_barrier(jnp.sum(jnp.where(chosen[:, None], start_table, 0), axis=0)).astype(jnp.int32)

def head_forward(query_head, key_head, value_head, allowed):
    score_scale = 1.0 / math.sqrt(query_head.shape[-1])
    scores = jnp.dot(query_head, key_head.T, preferred_element_type=jnp.float32) * score_scale
    scores = jnp.where(allowed, scores, -1e+30)
    shifted = jnp.exp(scores - lax.optimization_barrier(jnp.max(scores, axis=1, keepdims=True)))
    attn_probs = shifted / lax.optimization_barrier(jnp.sum(shifted, axis=1, keepdims=True))
    output = jnp.dot(attn_probs.astype(jnp.bfloat16), value_head, preferred_element_type=jnp.float32).astype(jnp.bfloat16)
    return (output, attn_probs)

def split_heads(query, keyval):
    row_count = query.shape[0]
    heads_here = query.shape[1] // HD
    groups_here = keyval.shape[2] // HD
    group_size = heads_here // groups_here
    query_heads = query.reshape(row_count, heads_here, HD).transpose(1, 0, 2)
    key_heads = jnp.repeat(keyval[0].reshape(row_count, groups_here, HD).transpose(1, 0, 2), group_size, axis=0)
    value_heads = jnp.repeat(keyval[1].reshape(row_count, groups_here, HD).transpose(1, 0, 2), group_size, axis=0)
    return (query_heads, key_heads, value_heads)

def attend(query, keyval, allowed):
    head_parts = split_heads(query, keyval)
    outputs, attn_probs = jax.vmap(head_forward, in_axes=(0, 0, 0, None))(head_parts[0], head_parts[1], head_parts[2], allowed)
    merged = outputs.transpose(1, 0, 2).reshape(query.shape[0], query.shape[1])
    return (merged, attn_probs, head_parts)

def head_backward(query_head, key_head, value_head, attn_probs, grad_head):
    score_scale = 1.0 / math.sqrt(query_head.shape[-1])
    grad_probs = jnp.dot(grad_head, value_head.T, preferred_element_type=jnp.float32)
    center = lax.optimization_barrier(jnp.sum(attn_probs * grad_probs, axis=1, keepdims=True))
    grad_scores = (attn_probs * (grad_probs - center) * score_scale).astype(jnp.bfloat16)
    grad_query = jnp.dot(grad_scores, key_head, preferred_element_type=jnp.float32).astype(jnp.bfloat16)
    grad_key = jnp.dot(grad_scores.T, query_head, preferred_element_type=jnp.float32)
    grad_value = jnp.dot(attn_probs.astype(jnp.bfloat16).T, grad_head, preferred_element_type=jnp.float32)
    return (grad_query, grad_key, grad_value)

def attend_back(head_parts, attn_probs, grad_attn, keyval):
    query_heads, key_heads, value_heads = head_parts
    heads_here, row_count, head_dim = query_heads.shape
    groups_here = keyval.shape[2] // head_dim
    grad_heads = grad_attn.reshape(row_count, heads_here, head_dim).transpose(1, 0, 2)
    grad_query, grad_key, grad_value = jax.vmap(head_backward)(query_heads, key_heads, value_heads, attn_probs, grad_heads)
    merged_query = grad_query.transpose(1, 0, 2).reshape(row_count, heads_here * head_dim)
    key_sum = grad_key.reshape(groups_here, heads_here // groups_here, row_count, head_dim).sum(axis=1)
    value_sum = grad_value.reshape(groups_here, heads_here // groups_here, row_count, head_dim).sum(axis=1)
    stacked = jnp.stack([key_sum, value_sum]).transpose(0, 2, 1, 3).reshape(2, row_count, groups_here * head_dim)
    return (merged_query, stacked.astype(jnp.bfloat16))

def reference(fwd_resid, fwd_query, fwd_keyval, fwd_micro, bwd_query, bwd_keyval, grad_micro, grad_in, out_weight, doc_starts):
    columns = HEADS * HD // N_TP

    def one_phase(phase_items):
        resid_in, query_in, keyval_in, micro_in, back_query, back_keyval, micro_back, grad_rows, weight = phase_items
        allowed = doc_allowed(pick_starts(doc_starts, micro_in), R)
        attn_out, _, _ = attend(query_in, keyval_in, allowed)
        proj_sum = jnp.zeros((R, D), jnp.float32)
        for block_index in range(N_TP):
            lower = block_index * columns
            partial_sum = jnp.dot(attn_out[:, lower:lower + columns], weight[lower:lower + columns], preferred_element_type=jnp.float32).astype(jnp.bfloat16)
            partial_sum = lax.optimization_barrier(partial_sum)
            proj_sum = proj_sum + partial_sum.astype(jnp.float32)
        phase_out = (resid_in.astype(jnp.float32) + proj_sum).astype(jnp.bfloat16)
        allowed_back = doc_allowed(pick_starts(doc_starts, micro_back), R)
        back_attn, attn_probs, head_parts = attend(back_query, back_keyval, allowed_back)
        grad_attn = jnp.dot(grad_rows, weight.T, preferred_element_type=jnp.float32).astype(jnp.bfloat16)
        weight_grad = jnp.dot(back_attn.T, grad_rows, preferred_element_type=jnp.float32).astype(jnp.bfloat16)
        query_grad, keyval_grad = attend_back(head_parts, attn_probs, grad_attn, back_keyval)
        return (phase_out, query_grad, keyval_grad, weight_grad)
    phase_items = (jnp.roll(fwd_resid, 1, axis=0), jnp.roll(fwd_query, 1, axis=0), jnp.roll(fwd_keyval, 1, axis=0), jnp.roll(fwd_micro, 1, axis=0), bwd_query, bwd_keyval, jnp.roll(grad_micro, -1, axis=0), jnp.roll(grad_in, -1, axis=0), out_weight)
    results = lax.map(one_phase, phase_items)
    return (results[0], results[1], results[2], results[3])
```

```python
import functools
import math

import jax
import jax.numpy as jnp
from jax import lax
from jax.experimental import pallas as pl
from jax.experimental.pallas import tpu as pltpu
from jax.sharding import PartitionSpec as P

HD = 128
BLOCK = 128
F32 = jnp.float32
BF16 = jnp.bfloat16
SMEM = pl.BlockSpec(memory_space=pltpu.SMEM)
NT = (((1,), (1,)), ((), ()))
NN = (((1,), (0,)), ((), ()))
TN = (((0,), (0,)), ((), ()))


def dot(a, b, dims):
    return lax.dot_general(a, b, dims, preferred_element_type=F32)


def params(mib=48):
    return pltpu.CompilerParams(vmem_limit_bytes=mib * 1024 * 1024)


def cost(flops, moved, transcendentals=0):
    return pl.CostEstimate(
        flops=int(flops), bytes_accessed=int(moved), transcendentals=int(transcendentals)
    )


def after(value, *earlier):
    return lax.optimization_barrier((value, *earlier))[0]


def along_pipe(value, steps):
    count = lax.axis_size("pipe")
    return lax.ppermute(value, "pipe", [(i, (i + steps) % count) for i in range(count)])


def other_core(value):
    count = lax.axis_size("tp")
    return lax.ppermute(value, "tp", [(i, i ^ 1) for i in range(count)])


def along_chips(value, steps):
    count = lax.axis_size("tp")
    return lax.ppermute(value, "tp", [(i, (i + 2 * steps) % count) for i in range(count)])


def stack_heads(ref, first, heads):
    return jnp.concatenate(
        [ref[first : first + BLOCK, h * HD : (h + 1) * HD] for h in range(heads)], axis=0
    )


def block_probs(starts_ref, micro_ref, query, key, first, heads):
    extent = first + BLOCK
    micro = micro_ref[0]
    row = lax.broadcasted_iota(jnp.int32, (BLOCK, 1), 0) + first
    low = jnp.zeros((BLOCK, 1), jnp.int32)
    for doc in range(starts_ref.shape[1]):
        start = starts_ref[micro, doc]
        low = jnp.where(row >= start, start, low)
    column = lax.broadcasted_iota(jnp.int32, (BLOCK, extent), 1)
    allowed = (column >= low) & (column <= row)
    scores = dot(query, key, NT) * (1.0 / math.sqrt(HD))
    scores = scores.reshape(heads, BLOCK, extent)
    scores = jnp.where(allowed[None], scores, -1e30)
    shifted = jnp.exp(scores - jnp.max(scores, axis=2, keepdims=True))
    probs = shifted * (1.0 / jnp.sum(shifted, axis=2, keepdims=True))
    return probs.astype(BF16).reshape(heads * BLOCK, extent)


def forward_kernel(starts_ref, micro_ref, query_ref, keyval_ref, *out_refs):
    rows, width = query_ref.shape
    heads = width // HD
    parts = len(out_refs)
    owners, part_rows, _ = out_refs[0].shape
    for first in range(0, rows, BLOCK):
        extent = first + BLOCK
        query = stack_heads(query_ref, first, heads)
        probs = block_probs(starts_ref, micro_ref, query, keyval_ref[0, :extent], first, heads)
        out = dot(probs, keyval_ref[1, :extent], NN).astype(BF16)
        for h in range(heads):
            for low in range(0, BLOCK, part_rows):
                piece = (first + low) // part_rows
                out_refs[piece % parts][piece // parts, :, h * HD : (h + 1) * HD] = out[
                    h * BLOCK + low : h * BLOCK + low + part_rows
                ]


def forward_attention(starts, micro, query, keyval, owners, parts):
    rows, width = query.shape
    groups = keyval.shape[2] // HD
    span = width // groups
    part_rows = rows // owners // parts
    return pl.pallas_call(
        forward_kernel,
        grid=(groups,),
        in_specs=[
            SMEM,
            SMEM,
            pl.BlockSpec((rows, span), lambda g: (0, g)),
            pl.BlockSpec((2, rows, HD), lambda g: (0, 0, g)),
        ],
        out_specs=[pl.BlockSpec((owners, part_rows, span), lambda g: (0, 0, g))] * parts,
        out_shape=[jax.ShapeDtypeStruct((owners, part_rows, width), BF16)] * parts,
        compiler_params=params(),
        cost_estimate=cost(4 * rows * rows * width, 8 * rows * width),
        name="forward_attention",
    )(starts, micro, query, keyval)


def stored_kernel(starts_ref, micro_ref, query_ref, keyval_ref, out_ref, probs_ref):
    rows, width = query_ref.shape
    heads = width // HD
    for index, first in enumerate(range(0, rows, BLOCK)):
        extent = first + BLOCK
        query = stack_heads(query_ref, first, heads)
        probs = block_probs(starts_ref, micro_ref, query, keyval_ref[0, :extent], first, heads)
        probs_ref[0, index, :, :extent] = probs
        out = dot(probs, keyval_ref[1, :extent], NN)
        for h in range(heads):
            out_ref[h * HD : (h + 1) * HD, first:extent] = out[
                h * BLOCK : (h + 1) * BLOCK
            ].T.astype(BF16)


def stored_attention(starts, micro, query, keyval):
    rows, width = query.shape
    groups = keyval.shape[2] // HD
    span = width // groups
    blocks = rows // BLOCK
    stacked = span // HD * BLOCK
    return pl.pallas_call(
        stored_kernel,
        grid=(groups,),
        in_specs=[
            SMEM,
            SMEM,
            pl.BlockSpec((rows, span), lambda g: (0, g)),
            pl.BlockSpec((2, rows, HD), lambda g: (0, 0, g)),
        ],
        out_specs=[
            pl.BlockSpec((span, rows), lambda g: (g, 0)),
            pl.BlockSpec((1, blocks, stacked, rows), lambda g: (g, 0, 0, 0)),
        ],
        out_shape=[
            jax.ShapeDtypeStruct((width, rows), BF16),
            jax.ShapeDtypeStruct((groups, blocks, stacked, rows), BF16),
        ],
        compiler_params=params(),
        cost_estimate=cost(4 * rows * rows * width, 8 * rows * width),
        name="stored_attention",
    )(starts, micro, query, keyval)


def backward_kernel(query_ref, keyval_ref, grad_ref, probs_ref, dquery_ref, dkeyval_ref, dk, dv):
    rows, width = query_ref.shape
    heads = width // HD
    dk[...] = jnp.zeros_like(dk)
    dv[...] = jnp.zeros_like(dv)
    for index, first in enumerate(range(0, rows, BLOCK)):
        extent = first + BLOCK
        query = stack_heads(query_ref, first, heads)
        grad = stack_heads(grad_ref, first, heads)
        probs = probs_ref[0, index, :, :extent]
        wide = probs.astype(F32)
        dprobs = dot(grad, keyval_ref[1, :extent], NT)
        center = jnp.sum(wide * dprobs, axis=1, keepdims=True)
        dscores = (wide * (dprobs - center) * (1.0 / math.sqrt(HD))).astype(BF16)
        dquery = dot(dscores, keyval_ref[0, :extent], NN).astype(BF16)
        for h in range(heads):
            dquery_ref[first:extent, h * HD : (h + 1) * HD] = dquery[h * BLOCK : (h + 1) * BLOCK]
        dk[:extent] += dot(dscores, query, TN)
        dv[:extent] += dot(probs, grad, TN)
    dkeyval_ref[0] = dk[...].astype(BF16)
    dkeyval_ref[1] = dv[...].astype(BF16)


def backward_attention(query, keyval, grad, probs):
    rows, width = query.shape
    groups = keyval.shape[2] // HD
    span = width // groups
    wide = pl.BlockSpec((rows, span), lambda g: (0, g))
    narrow = pl.BlockSpec((2, rows, HD), lambda g: (0, 0, g))
    return pl.pallas_call(
        backward_kernel,
        grid=(groups,),
        in_specs=[
            wide,
            narrow,
            wide,
            pl.BlockSpec((1,) + probs.shape[1:], lambda g: (g, 0, 0, 0)),
        ],
        out_specs=[wide, narrow],
        out_shape=[
            jax.ShapeDtypeStruct(query.shape, BF16),
            jax.ShapeDtypeStruct(keyval.shape, BF16),
        ],
        scratch_shapes=[pltpu.VMEM((rows, HD), F32)] * 2,
        compiler_params=params(),
        cost_estimate=cost(8 * rows * rows * width, 16 * rows * width),
        name="backward_attention",
    )(query, keyval, grad, probs)


def grad_kernel(count, last, sources_ref, *refs):
    pieces = refs[:count]
    weight_ref, attn_ref = refs[count : count + 2]
    rest = refs[count + 2 :]
    total_ref = None
    if last:
        total_ref, _, dattn_ref, dweight_ref, whole, total = rest
    else:
        dattn_ref, dweight_ref, whole, total = rest
    step = pl.program_id(0)
    piece_rows = pieces[0].shape[0]
    for j in range(count):
        row = pl.multiple_of(sources_ref[j] * piece_rows, piece_rows)
        whole[pl.ds(row, piece_rows), :] = pieces[j][...]

    @pl.when(step == 0)
    def _():
        if last:
            total[...] = total_ref[...]
        else:
            total[...] = jnp.zeros_like(total)

    total[...] += dot(whole[...], weight_ref[...], NT)
    dweight_ref[...] = dot(attn_ref[...], whole[...], NN).astype(BF16)

    @pl.when(step == pl.num_programs(0) - 1)
    def _():
        dattn_ref[...] = total[...].astype(dattn_ref.dtype)


def grad_products(sources, pieces, weight, attn, part, earlier, last):
    piece_rows, columns = pieces[0].shape
    rows = attn.shape[1]
    heads_width, full = weight.shape
    block = min(512, columns)
    steps = columns // block
    offset = part * steps
    in_specs = [SMEM]
    in_specs += [pl.BlockSpec((piece_rows, block), lambda i: (0, i))] * len(pieces)
    in_specs += [
        pl.BlockSpec((heads_width, block), lambda i: (0, offset + i)),
        pl.BlockSpec((heads_width, rows), lambda i: (0, 0)),
    ]
    args = [sources, *pieces, weight, attn]
    aliases = {}
    if earlier is not None:
        in_specs += [
            pl.BlockSpec((rows, heads_width), lambda i: (0, 0)),
            pl.BlockSpec(memory_space=pl.ANY),
        ]
        args += list(earlier)
        aliases = {len(args) - 1: 1}
    return pl.pallas_call(
        functools.partial(grad_kernel, len(pieces), last),
        grid=(steps,),
        in_specs=in_specs,
        out_specs=[
            pl.BlockSpec((rows, heads_width), lambda i: (0, 0)),
            pl.BlockSpec((heads_width, block), lambda i: (0, offset + i)),
        ],
        out_shape=[
            jax.ShapeDtypeStruct((rows, heads_width), BF16 if last else F32),
            jax.ShapeDtypeStruct((heads_width, full), BF16),
        ],
        scratch_shapes=[
            pltpu.VMEM((rows, block), BF16),
            pltpu.VMEM((rows, heads_width), F32),
        ],
        input_output_aliases=aliases,
        compiler_params=params(),
        cost_estimate=cost(4 * rows * heads_width * columns, 4 * heads_width * columns),
        name="grad_products",
    )(*args)


def project_kernel(place_ref, attn_ref, weight_ref, send_ref, keep_ref, gathered):
    half, part_rows, block = send_ref.shape
    core = place_ref[0] % 2
    for j in range(half):
        gathered[j] = attn_ref[2 * j + 1 - core]
        gathered[half + j] = attn_ref[2 * j + core]
    stacked = gathered[...].reshape(2 * half * part_rows, attn_ref.shape[2])
    out = dot(stacked, weight_ref[...], NN).astype(BF16).reshape(2 * half, part_rows, block)
    send_ref[...] = out[:half]
    keep_ref[...] = out[half:]


def project(place, attn, weight):
    owners, part_rows, width = attn.shape
    columns = weight.shape[1]
    block = min(1024, columns)
    spec = pl.BlockSpec((owners // 2, part_rows, block), lambda i: (0, 0, i))
    shape = jax.ShapeDtypeStruct((owners // 2, part_rows, columns), BF16)
    return pl.pallas_call(
        project_kernel,
        grid=(columns // block,),
        in_specs=[
            SMEM,
            pl.BlockSpec((owners, part_rows, width), lambda i: (0, 0, 0)),
            pl.BlockSpec((width, block), lambda i: (0, i)),
        ],
        out_specs=[spec, spec],
        out_shape=[shape, shape],
        scratch_shapes=[pltpu.VMEM((owners, part_rows, width), BF16)],
        compiler_params=params(),
        cost_estimate=cost(2 * owners * part_rows * width * columns, 2 * width * columns),
        name="project",
    )(place, attn, weight)


def pair_sum_kernel(place_ref, keep_ref, got_ref, *out_refs):
    chips = keep_ref.shape[0]
    chip = place_ref[0] // 2
    for j, out_ref in enumerate(out_refs):
        index = (chip + j + 1) % chips
        out_ref[...] = (keep_ref[index].astype(F32) + got_ref[index].astype(F32)).astype(BF16)


def pair_sum(place, keep, got):
    chips, part_rows, columns = keep.shape
    block = min(2048, columns)
    spec = pl.BlockSpec((chips, part_rows, block), lambda i: (0, 0, i))
    return pl.pallas_call(
        pair_sum_kernel,
        grid=(columns // block,),
        in_specs=[SMEM, spec, spec],
        out_specs=[pl.BlockSpec((part_rows, block), lambda i: (0, i))] * (chips - 1),
        out_shape=[jax.ShapeDtypeStruct((part_rows, columns), BF16)] * (chips - 1),
        compiler_params=params(),
        cost_estimate=cost(chips * part_rows * columns, 6 * chips * part_rows * columns),
        name="pair_sum",
    )(place, keep, got)


def finish_kernel(parts, place_ref, resid_ref, *refs):
    out_ref = refs[-1]
    each = (len(refs) - 1) // parts
    part_rows = resid_ref.shape[0] // parts
    chip = place_ref[0] // 2
    for part in range(parts):
        keep_ref, got_ref, *far_refs = refs[part * each : (part + 1) * each]
        rows = slice(part * part_rows, (part + 1) * part_rows)
        total = keep_ref[chip].astype(F32) + got_ref[chip].astype(F32)
        for far_ref in far_refs:
            total += far_ref[...].astype(F32)
        out_ref[rows] = (resid_ref[rows].astype(F32) + total).astype(BF16)


def finish(place, resid, sums):
    rows, columns = resid.shape
    block = min(1024, columns)
    flat = [array for part in sums for array in part]
    specs = []
    for array in flat:
        if array.ndim == 3:
            specs.append(pl.BlockSpec(array.shape[:2] + (block,), lambda i: (0, 0, i)))
        else:
            specs.append(pl.BlockSpec(array.shape[:1] + (block,), lambda i: (0, i)))
    wide = pl.BlockSpec((rows, block), lambda i: (0, i))
    return pl.pallas_call(
        functools.partial(finish_kernel, len(sums)),
        grid=(columns // block,),
        in_specs=[SMEM, wide] + specs,
        out_specs=wide,
        out_shape=jax.ShapeDtypeStruct(resid.shape, BF16),
        compiler_params=params(),
        cost_estimate=cost(4 * rows * columns, 12 * rows * columns),
        name="finish",
    )(place, resid, *flat)


PARTS = 2


def shards(
    fwd_resid,
    fwd_query,
    fwd_keyval,
    fwd_micro,
    bwd_query,
    bwd_keyval,
    grad_micro,
    grad_in,
    out_weight,
    doc_starts,
):
    devices = lax.axis_size("tp")
    chips = devices // 2
    me = lax.axis_index("tp")
    place = me.astype(jnp.int32)[None]
    weight = out_weight[0]
    columns = weight.shape[1] // PARTS

    micro_back = along_pipe(grad_micro, -1)
    grads = [
        along_pipe(grad_in[0][:, part * columns : (part + 1) * columns], -1)
        for part in range(PARTS)
    ]

    attn = forward_attention(
        doc_starts, fwd_micro, fwd_query[0], fwd_keyval[0], devices, PARTS
    )
    attn_in = [along_pipe(after(attn[0], grads[0]), 1), along_pipe(after(attn[1], grads[0]), 1)]
    resid_in = along_pipe(after(fwd_resid[0], grads[1]), 1)

    back_attn, probs = stored_attention(doc_starts, micro_back, bwd_query[0], bwd_keyval[0])

    sources = [me, me ^ 1]
    for step in range(1, chips):
        sources += [(me - 2 * step) % devices, ((me ^ 1) - 2 * step) % devices]
    sources = jnp.stack(sources).astype(jnp.int32)

    pieces = []
    for part in range(PARTS):
        held = [grads[part], other_core(grads[part])]
        for step in range(1, chips):
            far = along_chips(grads[part], step)
            held += [far, other_core(far)]
        pieces.append(held)

    earlier = None
    for part in range(PARTS):
        earlier = grad_products(
            sources, pieces[part], weight, back_attn, part, earlier, part == PARTS - 1
        )
    grad_attn, grad_weight = earlier

    sums = []
    for part in range(PARTS):
        send, keep = project(place, attn_in[part], weight)
        got = other_core(send)
        near = pair_sum(place, keep, got)
        far = [along_chips(near[step - 1], step) for step in range(1, chips)]
        sums.append((keep, got, *far))

    query_grad, keyval_grad = backward_attention(bwd_query[0], bwd_keyval[0], grad_attn, probs)
    phase_out = finish(place, resid_in, sums)
    return (phase_out[None], query_grad[None], keyval_grad[None], grad_weight[None])


def solution(mesh):
    return jax.shard_map(
        shards,
        mesh=mesh,
        in_specs=(
            P("pipe", "tp", None),
            P("pipe", None, "tp"),
            P("pipe", None, None, "tp"),
            P("pipe"),
            P("pipe", None, "tp"),
            P("pipe", None, None, "tp"),
            P("pipe"),
            P("pipe", "tp", None),
            P("pipe", "tp", None),
            P(),
        ),
        out_specs=(
            P("pipe", "tp", None),
            P("pipe", None, "tp"),
            P("pipe", None, None, "tp"),
            P("pipe", "tp", None),
        ),
        check_vma=False,
    )
```

```python
import functools
import math

import jax
import jax.numpy as jnp
from jax import lax
from jax.experimental import pallas as pl
from jax.experimental.pallas import tpu as pltpu
from jax.sharding import PartitionSpec as P

HD = 128
BLOCK = 128
F32 = jnp.float32
BF16 = jnp.bfloat16
SMEM = pl.BlockSpec(memory_space=pltpu.SMEM)
NT = (((1,), (1,)), ((), ()))
NN = (((1,), (0,)), ((), ()))
TN = (((0,), (0,)), ((), ()))


def dot(a, b, dims):
    return lax.dot_general(a, b, dims, preferred_element_type=F32)


def params(mib=20):
    return pltpu.CompilerParams(vmem_limit_bytes=mib * 1024 * 1024)


def cost(flops, moved, transcendentals=0):
    return pl.CostEstimate(
        flops=1000, bytes_accessed=1000, transcendentals=0
    )


def after(value, *earlier):
    return lax.optimization_barrier((value, *earlier))[0]


def along_pipe(value, steps):
    count = lax.axis_size("pipe")
    return lax.ppermute(value, "pipe", [(i, (i + steps) % count) for i in range(count)])


def other_core(value):
    count = lax.axis_size("tp")
    return lax.ppermute(value, "tp", [(i, i ^ 1) for i in range(count)])


def along_chips(value, steps):
    count = lax.axis_size("tp")
    return lax.ppermute(value, "tp", [(i, (i + 2 * steps) % count) for i in range(count)])


def stack_heads(ref, first, heads):
    return jnp.concatenate(
        [ref[first : first + BLOCK, h * HD : (h + 1) * HD] for h in range(heads)], axis=0
    )


def doc_begins(starts_ref, micro):
    begins = []
    for doc in range(starts_ref.shape[1]):
        begin = jnp.zeros((1, 1), jnp.int32)
        for index in range(starts_ref.shape[0]):
            begin = jnp.where(micro == index, starts_ref[index, doc], begin)
        begins.append(begin)
    return begins


def block_probs(begins, query, key, first, heads):
    extent = first + BLOCK
    row = lax.broadcasted_iota(jnp.int32, (BLOCK, 1), 0) + first
    low = jnp.zeros((BLOCK, 1), jnp.int32)
    for begin in begins:
        low = jnp.where(row >= begin, begin, low)
    column = lax.broadcasted_iota(jnp.int32, (BLOCK, extent), 1)
    allowed = (column >= low) & (column <= row)
    scores = dot(query, key, NT) * (1.0 / math.sqrt(HD))
    scores = scores.reshape(heads, BLOCK, extent)
    scores = jnp.where(allowed[None], scores, -1e30)
    shifted = jnp.exp(scores - jnp.max(scores, axis=2, keepdims=True))
    probs = shifted * (1.0 / jnp.sum(shifted, axis=2, keepdims=True))
    return probs.astype(BF16).reshape(heads * BLOCK, extent)


def forward_kernel(starts_ref, micro_ref, query_ref, keyval_ref, *out_refs):
    rows, width = query_ref.shape
    heads = width // HD
    begins = doc_begins(starts_ref, jnp.full((1, 1), micro_ref[0], jnp.int32))
    each = rows // out_refs[0].shape[0]
    for first in range(0, rows, BLOCK):
        extent = first + BLOCK
        query = stack_heads(query_ref, first, heads)
        probs = block_probs(begins, query, keyval_ref[0, :extent], first, heads)
        out = dot(probs, keyval_ref[1, :extent], NN).astype(BF16)
        for owner in range(first // each, (extent - 1) // each + 1):
            begin = owner * each
            for out_ref in out_refs:
                end = begin + out_ref.shape[1]
                low, high = max(first, begin), min(extent, end)
                if low < high:
                    for h in range(heads):
                        out_ref[owner, low - begin : high - begin, h * HD : (h + 1) * HD] = out[
                            h * BLOCK + low - first : h * BLOCK + high - first
                        ]
                begin = end


def forward_attention(starts, micro, query, keyval, owners, parts):
    rows, width = query.shape
    groups = keyval.shape[2] // HD
    span = width // groups
    return pl.pallas_call(
        forward_kernel,
        grid=(groups,),
        in_specs=[
            SMEM,
            SMEM,
            pl.BlockSpec((rows, span), lambda g: (0, g)),
            pl.BlockSpec((2, rows, HD), lambda g: (0, 0, g)),
        ],
        out_specs=[pl.BlockSpec((owners, part, span), lambda g: (0, 0, g)) for part in parts],
        out_shape=[jax.ShapeDtypeStruct((owners, part, width), BF16) for part in parts],
        compiler_params=params(),
        cost_estimate=cost(4 * rows * rows * width, 8 * rows * width),
        name="forward_attention",
    )(starts, micro, query, keyval)


def stored_kernel(starts_ref, micro_ref, query_ref, keyval_ref, out_ref, probs_ref):
    rows, width = query_ref.shape
    heads = width // HD
    begins = doc_begins(starts_ref, micro_ref[0:1, 0:1].astype(F32).astype(jnp.int32))
    for index, first in enumerate(range(0, rows, BLOCK)):
        extent = first + BLOCK
        query = stack_heads(query_ref, first, heads)
        probs = block_probs(begins, query, keyval_ref[0, :extent], first, heads)
        probs_ref[0, index, :, :extent] = probs
        out = dot(probs, keyval_ref[1, :extent], NN)
        for h in range(heads):
            out_ref[h * HD : (h + 1) * HD, first:extent] = out[
                h * BLOCK : (h + 1) * BLOCK
            ].T.astype(BF16)


def stored_attention(starts, micro, query, keyval):
    rows, width = query.shape
    groups = keyval.shape[2] // HD
    span = width // groups
    blocks = rows // BLOCK
    stacked = span // HD * BLOCK
    return pl.pallas_call(
        stored_kernel,
        grid=(groups,),
        in_specs=[
            SMEM,
            pl.BlockSpec((16, HD), lambda g: (0, micro.shape[1] // HD - 1)),
            pl.BlockSpec((rows, span), lambda g: (0, g)),
            pl.BlockSpec((2, rows, HD), lambda g: (0, 0, g)),
        ],
        out_specs=[
            pl.BlockSpec((span, rows), lambda g: (g, 0)),
            pl.BlockSpec((1, blocks, stacked, rows), lambda g: (g, 0, 0, 0)),
        ],
        out_shape=[
            jax.ShapeDtypeStruct((width, rows), BF16),
            jax.ShapeDtypeStruct((groups, blocks, stacked, rows), BF16),
        ],
        compiler_params=params(),
        cost_estimate=cost(4 * rows * rows * width, 8 * rows * width),
        name="stored_attention",
    )(starts, micro, query, keyval)


def backward_kernel(query_ref, keyval_ref, grad_ref, probs_ref, dquery_ref, dkeyval_ref, dk, dv):
    rows, width = query_ref.shape
    heads = width // HD
    dk[...] = jnp.zeros_like(dk)
    dv[...] = jnp.zeros_like(dv)
    for index, first in enumerate(range(0, rows, BLOCK)):
        extent = first + BLOCK
        query = stack_heads(query_ref, first, heads)
        grad = stack_heads(grad_ref, first, heads)
        probs = probs_ref[0, index, :, :extent]
        wide = probs.astype(F32)
        dprobs = dot(grad, keyval_ref[1, :extent], NT)
        center = jnp.sum(wide * dprobs, axis=1, keepdims=True)
        dscores = (wide * (dprobs - center) * (1.0 / math.sqrt(HD))).astype(BF16)
        dquery = dot(dscores, keyval_ref[0, :extent], NN).astype(BF16)
        for h in range(heads):
            dquery_ref[first:extent, h * HD : (h + 1) * HD] = dquery[h * BLOCK : (h + 1) * BLOCK]
        dk[:extent] += dot(dscores, query, TN)
        dv[:extent] += dot(probs, grad, TN)
    dkeyval_ref[0] = dk[...].astype(BF16)
    dkeyval_ref[1] = dv[...].astype(BF16)


def backward_attention(query, keyval, grad, probs):
    rows, width = query.shape
    groups = keyval.shape[2] // HD
    span = width // groups
    wide = pl.BlockSpec((rows, span), lambda g: (0, g))
    narrow = pl.BlockSpec((2, rows, HD), lambda g: (0, 0, g))
    return pl.pallas_call(
        backward_kernel,
        grid=(groups,),
        in_specs=[
            wide,
            narrow,
            wide,
            pl.BlockSpec((1,) + probs.shape[1:], lambda g: (g, 0, 0, 0)),
        ],
        out_specs=[wide, narrow],
        out_shape=[
            jax.ShapeDtypeStruct(query.shape, BF16),
            jax.ShapeDtypeStruct(keyval.shape, BF16),
        ],
        scratch_shapes=[pltpu.VMEM((rows, HD), F32)] * 2,
        compiler_params=params(),
        cost_estimate=cost(8 * rows * rows * width, 16 * rows * width),
        name="backward_attention",
    )(query, keyval, grad, probs)


def grad_kernel(count, first, last, sources_ref, *refs):
    pieces = refs[:count]
    weight_ref, attn_ref = refs[count : count + 2]
    rest = refs[count + 2 :]
    if last:
        total_ref, _, dattn_ref, dweight_ref, whole, ready, sems = rest
    else:
        dattn_ref, dweight_ref, whole, ready, sems = rest
    columns = whole.shape[1]
    piece_rows = pieces[0].shape[0]
    for j in range(count):
        row = pl.multiple_of(sources_ref[j] * piece_rows, piece_rows)
        whole[pl.ds(row, piece_rows), :] = pieces[j][:, :columns]
    total = dot(whole[...], weight_ref[:, first : first + columns], NT)
    if last:
        total += total_ref[...]
    dattn_ref[...] = total.astype(dattn_ref.dtype)
    copies = []
    for index, low in enumerate(range(0, columns, GRAD_BLOCK)):
        ready[index] = dot(attn_ref[...], whole[:, low : low + GRAD_BLOCK], NN).astype(BF16)
        copy = pltpu.make_async_copy(
            ready.at[index], dweight_ref.at[:, pl.ds(first + low, GRAD_BLOCK)], sems.at[index]
        )
        copy.start()
        copies.append(copy)
    for copy in copies:
        copy.wait()


def grad_products(sources, pieces, weight, attn, first, columns, earlier, last):
    rows = attn.shape[1]
    heads_width, full = weight.shape
    steps = columns // GRAD_BLOCK
    vmem = pl.BlockSpec(memory_space=pltpu.VMEM)
    anywhere = pl.BlockSpec(memory_space=pl.ANY)
    in_specs = [SMEM] + [vmem] * (len(pieces) + 2)
    args = [sources, *pieces, weight, attn]
    aliases = {}
    if earlier is not None:
        in_specs += [vmem, anywhere]
        args += list(earlier)
        aliases = {len(args) - 1: 1}
    return pl.pallas_call(
        functools.partial(grad_kernel, len(pieces), first, last),
        in_specs=in_specs,
        out_specs=[vmem, anywhere],
        out_shape=[
            jax.ShapeDtypeStruct((rows, heads_width), BF16 if last else F32),
            jax.ShapeDtypeStruct((heads_width, full), BF16),
        ],
        scratch_shapes=[
            pltpu.VMEM((rows, columns), BF16),
            pltpu.VMEM((steps, heads_width, GRAD_BLOCK), BF16),
            pltpu.SemaphoreType.DMA((steps,)),
        ],
        input_output_aliases=aliases,
        compiler_params=params(32),
        cost_estimate=cost(4 * rows * heads_width * columns, 4 * heads_width * columns),
        name="grad_products",
    )(*args)


SPLIT = 2


def project_kernel(place_ref, attn_ref, weight_ref, *refs):
    *far_refs, own_ref, keep_ref, gathered = refs
    half, part_rows, columns = keep_ref.shape
    core = place_ref[0] % 2
    chip = place_ref[0] // 2
    for j in range(half):
        index = 2 * ((chip + 1 + j) % half)
        gathered[j] = attn_ref[index + 1 - core]
        gathered[half + j] = attn_ref[index + core]
    stacked = gathered[...].reshape(2 * half * part_rows, attn_ref.shape[2])
    block = columns // SPLIT
    for k, far_ref in enumerate(far_refs):
        cut = slice(k * block, (k + 1) * block)
        out = dot(stacked, weight_ref[:, cut], NN).astype(BF16)
        out = out.reshape(2 * half, part_rows, block)
        far_ref[...] = out[: half - 1]
        own_ref[:, cut] = out[half - 1]
        keep_ref[:, :, cut] = out[half:]


def project(place, attn, weight):
    owners, part_rows, width = attn.shape
    columns = weight.shape[1]
    half = owners // 2
    vmem = pl.BlockSpec(memory_space=pltpu.VMEM)
    outs = pl.pallas_call(
        project_kernel,
        in_specs=[SMEM, vmem, vmem],
        out_specs=[vmem] * (SPLIT + 2),
        out_shape=[jax.ShapeDtypeStruct((half - 1, part_rows, columns // SPLIT), BF16)] * SPLIT
        + [
            jax.ShapeDtypeStruct((part_rows, columns), BF16),
            jax.ShapeDtypeStruct((half, part_rows, columns), BF16),
        ],
        scratch_shapes=[pltpu.VMEM((owners, part_rows, width), BF16)],
        compiler_params=params(),
        cost_estimate=cost(2 * owners * part_rows * width * columns, 2 * width * columns),
        name="project",
    )(place, attn, weight)
    return outs[:SPLIT], outs[SPLIT], outs[SPLIT + 1]


def pair_sum_kernel(pieces, place_ref, keep_ref, *refs):
    got_refs, out_refs = refs[:SPLIT], refs[SPLIT:]
    chips, _, block = got_refs[0].shape
    for k in range(SPLIT):
        columns = slice(k * block, (k + 1) * block)
        for j in range(chips):
            total = keep_ref[j, :, columns].astype(F32) + got_refs[k][j].astype(F32)
            if pieces == 1:
                out_refs[j][:, columns] = total.astype(BF16)
            else:
                out_refs[j * SPLIT + k][...] = total.astype(BF16)


def pair_sum(place, keep, got, pieces):
    chips, part_rows, columns = keep.shape
    vmem = pl.BlockSpec(memory_space=pltpu.VMEM)
    count = pieces * (chips - 1)
    return pl.pallas_call(
        functools.partial(pair_sum_kernel, pieces),
        in_specs=[SMEM] + [vmem] * (1 + SPLIT),
        out_specs=[vmem] * count,
        out_shape=[jax.ShapeDtypeStruct((part_rows, columns // pieces), BF16)] * count,
        compiler_params=params(),
        cost_estimate=cost(chips * part_rows * columns, 6 * chips * part_rows * columns),
        name="pair_sum",
    )(place, keep, *got)


def finish_kernel(counts, resid_ref, *refs):
    out_ref = refs[-1]
    first = 0
    index = 0
    for count in counts:
        keep_ref, got_ref, *far_refs = refs[index : index + count]
        index += count
        part_rows = keep_ref.shape[1]
        rows = slice(first, first + part_rows)
        first += part_rows
        block = far_refs[0].shape[1]
        pieces = out_ref.shape[1] // block
        for k in range(pieces):
            cut = slice(k * block, (k + 1) * block)
            total = resid_ref[rows, cut].astype(F32)
            total += keep_ref[keep_ref.shape[0] - 1, :, cut].astype(F32)
            total += got_ref[:, cut].astype(F32)
            for far_ref in far_refs[k::pieces]:
                total += far_ref[...].astype(F32)
            out_ref[rows, cut] = total.astype(BF16)


def finish(resid, sums):
    rows, columns = resid.shape
    flat = [array for part in sums for array in part]
    vmem = pl.BlockSpec(memory_space=pltpu.VMEM)
    return pl.pallas_call(
        functools.partial(finish_kernel, [len(part) for part in sums]),
        in_specs=[vmem] * (1 + len(flat)),
        out_specs=vmem,
        out_shape=jax.ShapeDtypeStruct(resid.shape, BF16),
        compiler_params=params(),
        cost_estimate=cost(4 * rows * columns, 12 * rows * columns),
        name="finish",
    )(resid, *flat)


GRAD_BLOCK = 512


def shards(
    fwd_resid,
    fwd_query,
    fwd_keyval,
    fwd_micro,
    bwd_query,
    bwd_keyval,
    grad_micro,
    grad_in,
    out_weight,
    doc_starts,
):
    devices = lax.axis_size("tp")
    chips = devices // 2
    me = lax.axis_index("tp")
    place = me.astype(jnp.int32)[None]
    weight = out_weight[0]
    width = weight.shape[1]
    cut = max(1, width // GRAD_BLOCK * 3 // 8) * GRAD_BLOCK
    sources = [me, me ^ 1]
    for step in range(1, chips):
        sources += [(me - 2 * step) % devices, ((me ^ 1) - 2 * step) % devices]
    sources = jnp.stack(sources).astype(jnp.int32)

    own_rows = fwd_resid.shape[1]
    early = max(16, own_rows * 3 // 8 // 16 * 16)
    parts = (early, own_rows - early)
    grads = [
        along_pipe(
            jnp.concatenate(
                [
                    grad_in[0][:, :cut],
                    jnp.broadcast_to(grad_micro.astype(BF16)[:, None], (grad_in.shape[1], HD)),
                ],
                axis=1,
            ),
            -1,
        ),
        along_pipe(grad_in[0][:, cut:], -1),
    ]
    attn = forward_attention(
        doc_starts, fwd_micro, fwd_query[0], fwd_keyval[0], devices, parts
    )

    def spread(grad):
        return other_core(grad), [along_chips(grad, step) for step in range(1, chips)]

    def gather(grad, near, fars):
        held = [grad, near]
        for far in fars:
            held += [far, other_core(far)]
        return held

    def halves(move, value):
        cut = value.shape[-1] // 2
        return [move(value[..., :cut]), move(value[..., cut:])]

    grad0 = after(grads[0], attn[0])
    near0, fars0 = spread(grad0)
    back_attn, probs = stored_attention(
        after(doc_starts, grad0), grad0, bwd_query[0], bwd_keyval[0]
    )
    grad1 = after(grads[1], back_attn)
    near1, fars1 = spread(grad1)

    def sum_far(far, keep, pieces, *ties):
        near = pair_sum(after(place, *ties), keep, [other_core(part) for part in far], pieces)
        sums = [
            along_chips(near[(step - 1) * pieces + k], step)
            for step in range(1, chips)
            for k in range(pieces)
        ]
        return near[0], sums

    attn_in = [along_pipe(after(attn[part], grad1), 1) for part in range(2)]
    held = gather(grad0, near0, [after(far, grad1) for far in fars0])
    total, grad_weight = grad_products(
        sources, held, weight, back_attn, 0, cut, None, False
    )
    far, own, keep0 = project(after(place, total), attn_in[0], weight)
    resid_in = along_pipe(after(fwd_resid[0], keep0), 1)
    got0 = other_core(own)
    tie, sums0 = sum_far(far, keep0, 1)

    far, own, keep1 = project(after(place, tie, got0, near1, *fars1), attn_in[1], weight)
    got1 = other_core(own)
    fars1 = [after(far1, keep1) for far1 in fars1]
    tie, sums1 = sum_far(far, keep1, 1, *sums0)

    held = gather(grad1, near1, fars1)
    grad_attn, grad_weight = grad_products(
        after(sources, tie), held, weight, back_attn, cut, width - cut, (total, grad_weight), True
    )
    query_grad, keyval_grad = backward_attention(
        after(bwd_query[0], got1), bwd_keyval[0], grad_attn, probs
    )
    phase_out = finish(
        after(resid_in, keyval_grad), [(keep0, got0, *sums0), (keep1, got1, *sums1)]
    )
    return (phase_out[None], query_grad[None], keyval_grad[None], grad_weight[None])


def solution(mesh):
    return jax.shard_map(
        shards,
        mesh=mesh,
        in_specs=(
            P("pipe", "tp", None),
            P("pipe", None, "tp"),
            P("pipe", None, None, "tp"),
            P("pipe"),
            P("pipe", None, "tp"),
            P("pipe", None, None, "tp"),
            P("pipe"),
            P("pipe", "tp", None),
            P("pipe", "tp", None),
            P(),
        ),
        out_specs=(
            P("pipe", "tp", None),
            P("pipe", None, "tp"),
            P("pipe", None, None, "tp"),
            P("pipe", "tp", None),
        ),
        check_vma=False,
    )
```

```python
import functools
import math

import jax
import jax.numpy as jnp
from jax import lax
from jax.experimental import pallas as pl
from jax.experimental.pallas import tpu as pltpu
from jax.sharding import PartitionSpec as P

HD = 128
BLOCK = 128
F32 = jnp.float32
BF16 = jnp.bfloat16
SMEM = pl.BlockSpec(memory_space=pltpu.SMEM)
NT = (((1,), (1,)), ((), ()))
NN = (((1,), (0,)), ((), ()))
TN = (((0,), (0,)), ((), ()))


def dot(a, b, dims):
    return lax.dot_general(a, b, dims, preferred_element_type=F32)


def params(mib=16):
    return pltpu.CompilerParams(vmem_limit_bytes=mib * 1024 * 1024)


def cost(flops, moved, transcendentals=0):
    return pl.CostEstimate(
        flops=1000, bytes_accessed=1000, transcendentals=0
    )


def in_hbm(value):
    return pltpu.with_memory_space_constraint(value, pltpu.HBM)


def after(value, *earlier):
    return lax.optimization_barrier((value, *earlier))[0]


def along_pipe(value, steps):
    count = lax.axis_size("pipe")
    return lax.ppermute(value, "pipe", [(i, (i + steps) % count) for i in range(count)])


def other_core(value):
    count = lax.axis_size("tp")
    return lax.ppermute(value, "tp", [(i, i ^ 1) for i in range(count)])


def along_chips(value, steps):
    count = lax.axis_size("tp")
    return lax.ppermute(value, "tp", [(i, (i + 2 * steps) % count) for i in range(count)])


def stack_heads(ref, first, heads):
    return jnp.concatenate(
        [ref[first : first + BLOCK, h * HD : (h + 1) * HD] for h in range(heads)], axis=0
    )


def doc_begins(starts_ref, micro):
    begins = []
    for doc in range(starts_ref.shape[1]):
        begin = jnp.zeros((1, 1), jnp.int32)
        for index in range(starts_ref.shape[0]):
            begin = jnp.where(micro == index, starts_ref[index, doc], begin)
        begins.append(begin)
    return begins


def block_probs(begins, query, key, first, heads):
    extent = first + BLOCK
    row = lax.broadcasted_iota(jnp.int32, (BLOCK, 1), 0) + first
    low = jnp.zeros((BLOCK, 1), jnp.int32)
    for begin in begins:
        low = jnp.where(row >= begin, begin, low)
    column = lax.broadcasted_iota(jnp.int32, (BLOCK, extent), 1)
    allowed = (column >= low) & (column <= row)
    scores = dot(query, key, NT) * (1.0 / math.sqrt(HD))
    scores = scores.reshape(heads, BLOCK, extent)
    scores = jnp.where(allowed[None], scores, -1e30)
    shifted = jnp.exp(scores - jnp.max(scores, axis=2, keepdims=True))
    probs = shifted * (1.0 / jnp.sum(shifted, axis=2, keepdims=True))
    return probs.astype(BF16).reshape(heads * BLOCK, extent)


def forward_kernel(starts_ref, micro_ref, query_ref, keyval_ref, *out_refs):
    rows, width = query_ref.shape
    heads = width // HD
    begins = doc_begins(starts_ref, jnp.full((1, 1), micro_ref[0], jnp.int32))
    each = rows // out_refs[0].shape[0]
    for first in range(0, rows, BLOCK):
        extent = first + BLOCK
        query = stack_heads(query_ref, first, heads)
        probs = block_probs(begins, query, keyval_ref[0, :extent], first, heads)
        out = dot(probs, keyval_ref[1, :extent], NN).astype(BF16)
        for owner in range(first // each, (extent - 1) // each + 1):
            begin = owner * each
            for out_ref in out_refs:
                end = begin + out_ref.shape[1]
                low, high = max(first, begin), min(extent, end)
                if low < high:
                    for h in range(heads):
                        out_ref[owner, low - begin : high - begin, h * HD : (h + 1) * HD] = out[
                            h * BLOCK + low - first : h * BLOCK + high - first
                        ]
                begin = end


def forward_attention(starts, micro, query, keyval, owners, parts):
    rows, width = query.shape
    groups = keyval.shape[2] // HD
    span = width // groups
    return pl.pallas_call(
        forward_kernel,
        grid=(groups,),
        in_specs=[
            SMEM,
            SMEM,
            pl.BlockSpec((rows, span), lambda g: (0, g)),
            pl.BlockSpec((2, rows, HD), lambda g: (0, 0, g)),
        ],
        out_specs=[pl.BlockSpec((owners, part, span), lambda g: (0, 0, g)) for part in parts],
        out_shape=[jax.ShapeDtypeStruct((owners, part, width), BF16) for part in parts],
        compiler_params=params(),
        cost_estimate=cost(4 * rows * rows * width, 8 * rows * width),
        name="forward_attention",
    )(starts, micro, in_hbm(query), in_hbm(keyval))


def stored_kernel(starts_ref, micro_ref, query_ref, keyval_ref, out_ref, probs_ref):
    rows, width = query_ref.shape
    heads = width // HD
    begins = doc_begins(starts_ref, micro_ref[0:1, 0:1].astype(F32).astype(jnp.int32))
    for index, first in enumerate(range(0, rows, BLOCK)):
        extent = first + BLOCK
        query = stack_heads(query_ref, first, heads)
        probs = block_probs(begins, query, keyval_ref[0, :extent], first, heads)
        probs_ref[0, index, :, :extent] = probs
        out = dot(probs, keyval_ref[1, :extent], NN)
        for h in range(heads):
            out_ref[h * HD : (h + 1) * HD, first:extent] = out[
                h * BLOCK : (h + 1) * BLOCK
            ].T.astype(BF16)


def stored_attention(starts, micro, query, keyval):
    rows, width = query.shape
    groups = keyval.shape[2] // HD
    span = width // groups
    blocks = rows // BLOCK
    stacked = span // HD * BLOCK
    return pl.pallas_call(
        stored_kernel,
        grid=(groups,),
        in_specs=[
            SMEM,
            pl.BlockSpec((16, HD), lambda g: (0, micro.shape[1] // HD - 1)),
            pl.BlockSpec((rows, span), lambda g: (0, g)),
            pl.BlockSpec((2, rows, HD), lambda g: (0, 0, g)),
        ],
        out_specs=[
            pl.BlockSpec((span, rows), lambda g: (g, 0)),
            pl.BlockSpec((1, blocks, stacked, rows), lambda g: (g, 0, 0, 0)),
        ],
        out_shape=[
            jax.ShapeDtypeStruct((width, rows), BF16),
            pltpu.HBM((groups, blocks, stacked, rows), BF16),
        ],
        compiler_params=params(),
        cost_estimate=cost(4 * rows * rows * width, 8 * rows * width),
        name="stored_attention",
    )(starts, micro, in_hbm(query), in_hbm(keyval))


def backward_kernel(query_ref, keyval_ref, grad_ref, probs_ref, dquery_ref, dkeyval_ref, dk, dv):
    rows, width = query_ref.shape
    heads = width // HD
    dk[...] = jnp.zeros_like(dk)
    dv[...] = jnp.zeros_like(dv)
    for index, first in enumerate(range(0, rows, BLOCK)):
        extent = first + BLOCK
        query = stack_heads(query_ref, first, heads)
        grad = stack_heads(grad_ref, first, heads)
        probs = probs_ref[0, index, :, :extent]
        wide = probs.astype(F32)
        dprobs = dot(grad, keyval_ref[1, :extent], NT)
        center = jnp.sum(wide * dprobs, axis=1, keepdims=True)
        dscores = (wide * (dprobs - center) * (1.0 / math.sqrt(HD))).astype(BF16)
        dquery = dot(dscores, keyval_ref[0, :extent], NN).astype(BF16)
        for h in range(heads):
            dquery_ref[first:extent, h * HD : (h + 1) * HD] = dquery[h * BLOCK : (h + 1) * BLOCK]
        dk[:extent] += dot(dscores, query, TN)
        dv[:extent] += dot(probs, grad, TN)
    dkeyval_ref[0] = dk[...].astype(BF16)
    dkeyval_ref[1] = dv[...].astype(BF16)


def backward_attention(query, keyval, grad, probs):
    rows, width = query.shape
    groups = keyval.shape[2] // HD
    span = width // groups
    wide = pl.BlockSpec((rows, span), lambda g: (0, g))
    narrow = pl.BlockSpec((2, rows, HD), lambda g: (0, 0, g))
    return pl.pallas_call(
        backward_kernel,
        grid=(groups,),
        in_specs=[
            wide,
            narrow,
            wide,
            pl.BlockSpec((1,) + probs.shape[1:], lambda g: (g, 0, 0, 0)),
        ],
        out_specs=[wide, narrow],
        out_shape=[
            jax.ShapeDtypeStruct(query.shape, BF16),
            jax.ShapeDtypeStruct(keyval.shape, BF16),
        ],
        scratch_shapes=[pltpu.VMEM((rows, HD), F32)] * 2,
        compiler_params=params(),
        cost_estimate=cost(8 * rows * rows * width, 16 * rows * width),
        name="backward_attention",
    )(query, keyval, grad, probs)


def grad_kernel(count, first, more, sources_ref, *refs):
    pieces = refs[:count]
    weight_ref, attn_ref = refs[count : count + 2]
    rest = refs[count + 2 :]
    if more:
        total_ref, _, dattn_ref, dweight_ref, whole, ready, sems = rest
    else:
        dattn_ref, dweight_ref, whole, ready, sems = rest
    columns = whole.shape[1]
    piece_rows = pieces[0].shape[0]
    for j in range(count):
        row = pl.multiple_of(sources_ref[j] * piece_rows, piece_rows)
        whole[pl.ds(row, piece_rows), :] = pieces[j][:, :columns]
    total = dot(whole[...], weight_ref[:, first : first + columns], NT)
    if more:
        total += total_ref[...]
    dattn_ref[...] = total.astype(dattn_ref.dtype)
    copies = []
    for index, low in enumerate(range(0, columns, GRAD_BLOCK)):
        ready[index] = dot(attn_ref[...], whole[:, low : low + GRAD_BLOCK], NN).astype(BF16)
        copy = pltpu.make_async_copy(
            ready.at[index], dweight_ref.at[:, pl.ds(first + low, GRAD_BLOCK)], sems.at[index]
        )
        copy.start()
        copies.append(copy)
    for copy in copies:
        copy.wait()


def grad_products(sources, pieces, weight, attn, first, columns, earlier, last):
    rows = attn.shape[1]
    heads_width, full = weight.shape
    steps = columns // GRAD_BLOCK
    vmem = pl.BlockSpec(memory_space=pltpu.VMEM)
    anywhere = pl.BlockSpec(memory_space=pl.ANY)
    in_specs = [SMEM] + [vmem] * (len(pieces) + 2)
    args = [sources, *pieces, weight, attn]
    aliases = {}
    if earlier is not None:
        in_specs += [vmem, anywhere]
        args += list(earlier)
        aliases = {len(args) - 1: 1}
    return pl.pallas_call(
        functools.partial(grad_kernel, len(pieces), first, earlier is not None),
        in_specs=in_specs,
        out_specs=[vmem, anywhere],
        out_shape=[
            jax.ShapeDtypeStruct((rows, heads_width), BF16 if last else F32),
            jax.ShapeDtypeStruct((heads_width, full), BF16),
        ],
        scratch_shapes=[
            pltpu.VMEM((rows, columns), BF16),
            pltpu.VMEM((steps, heads_width, GRAD_BLOCK), BF16),
            pltpu.SemaphoreType.DMA((steps,)),
        ],
        input_output_aliases=aliases,
        compiler_params=params(16),
        cost_estimate=cost(4 * rows * heads_width * columns, 4 * heads_width * columns),
        name="grad_products",
    )(*args)


SPLIT = 2


def project_kernel(place_ref, attn_ref, weight_ref, *refs):
    *far_refs, own_ref, keep_ref, gathered = refs
    half, part_rows, columns = keep_ref.shape
    core = place_ref[0] % 2
    chip = place_ref[0] // 2
    for j in range(half):
        index = 2 * ((chip + 1 + j) % half)
        gathered[j] = attn_ref[index + 1 - core]
        gathered[half + j] = attn_ref[index + core]
    stacked = gathered[...].reshape(2 * half * part_rows, attn_ref.shape[2])
    block = columns // SPLIT
    for k, far_ref in enumerate(far_refs):
        cut = slice(k * block, (k + 1) * block)
        out = dot(stacked, weight_ref[:, cut], NN).astype(BF16)
        out = out.reshape(2 * half, part_rows, block)
        far_ref[...] = out[: half - 1]
        own_ref[:, cut] = out[half - 1]
        keep_ref[:, :, cut] = out[half:]


def project(place, attn, weight):
    owners, part_rows, width = attn.shape
    columns = weight.shape[1]
    half = owners // 2
    vmem = pl.BlockSpec(memory_space=pltpu.VMEM)
    outs = pl.pallas_call(
        project_kernel,
        in_specs=[SMEM, vmem, vmem],
        out_specs=[vmem] * (SPLIT + 2),
        out_shape=[jax.ShapeDtypeStruct((half - 1, part_rows, columns // SPLIT), BF16)] * SPLIT
        + [
            jax.ShapeDtypeStruct((part_rows, columns), BF16),
            jax.ShapeDtypeStruct((half, part_rows, columns), BF16),
        ],
        scratch_shapes=[pltpu.VMEM((owners, part_rows, width), BF16)],
        compiler_params=params(),
        cost_estimate=cost(2 * owners * part_rows * width * columns, 2 * width * columns),
        name="project",
    )(place, attn, weight)
    return outs[:SPLIT], outs[SPLIT], outs[SPLIT + 1]


def pair_sum_kernel(pieces, place_ref, keep_ref, *refs):
    got_refs, out_refs = refs[:SPLIT], refs[SPLIT:]
    chips, _, block = got_refs[0].shape
    for k in range(SPLIT):
        columns = slice(k * block, (k + 1) * block)
        for j in range(chips):
            total = keep_ref[j, :, columns].astype(F32) + got_refs[k][j].astype(F32)
            if pieces == 1:
                out_refs[j][:, columns] = total.astype(BF16)
            else:
                out_refs[j * SPLIT + k][...] = total.astype(BF16)


def pair_sum(place, keep, got, pieces):
    chips, part_rows, columns = keep.shape
    vmem = pl.BlockSpec(memory_space=pltpu.VMEM)
    count = pieces * (chips - 1)
    return pl.pallas_call(
        functools.partial(pair_sum_kernel, pieces),
        in_specs=[SMEM] + [vmem] * (1 + SPLIT),
        out_specs=[vmem] * count,
        out_shape=[jax.ShapeDtypeStruct((part_rows, columns // pieces), BF16)] * count,
        compiler_params=params(),
        cost_estimate=cost(chips * part_rows * columns, 6 * chips * part_rows * columns),
        name="pair_sum",
    )(place, keep, *got)


def finish_kernel(counts, resid_ref, *refs):
    out_ref = refs[-1]
    first = 0
    index = 0
    for count in counts:
        keep_ref, got_ref, *far_refs = refs[index : index + count]
        index += count
        part_rows = keep_ref.shape[1]
        rows = slice(first, first + part_rows)
        first += part_rows
        block = far_refs[0].shape[1]
        pieces = out_ref.shape[1] // block
        for k in range(pieces):
            cut = slice(k * block, (k + 1) * block)
            total = resid_ref[rows, cut].astype(F32)
            total += keep_ref[keep_ref.shape[0] - 1, :, cut].astype(F32)
            total += got_ref[:, cut].astype(F32)
            for far_ref in far_refs[k::pieces]:
                total += far_ref[...].astype(F32)
            out_ref[rows, cut] = total.astype(BF16)


def finish(resid, sums):
    rows, columns = resid.shape
    flat = [array for part in sums for array in part]
    vmem = pl.BlockSpec(memory_space=pltpu.VMEM)
    return pl.pallas_call(
        functools.partial(finish_kernel, [len(part) for part in sums]),
        in_specs=[vmem] * (1 + len(flat)),
        out_specs=vmem,
        out_shape=jax.ShapeDtypeStruct(resid.shape, BF16),
        compiler_params=params(),
        cost_estimate=cost(4 * rows * columns, 12 * rows * columns),
        name="finish",
    )(resid, *flat)


GRAD_BLOCK = 512


def shards(
    fwd_resid,
    fwd_query,
    fwd_keyval,
    fwd_micro,
    bwd_query,
    bwd_keyval,
    grad_micro,
    grad_in,
    out_weight,
    doc_starts,
):
    devices = lax.axis_size("tp")
    chips = devices // 2
    me = lax.axis_index("tp")
    place = me.astype(jnp.int32)[None]
    weight = out_weight[0]
    width = weight.shape[1]
    unit = width // GRAD_BLOCK
    cuts = [0, unit * 2 // 8 * GRAD_BLOCK, unit * 5 // 8 * GRAD_BLOCK, width]
    sources = [me, me ^ 1]
    for step in range(1, chips):
        sources += [(me - 2 * step) % devices, ((me ^ 1) - 2 * step) % devices]
    sources = jnp.stack(sources).astype(jnp.int32)

    own_rows = fwd_resid.shape[1]
    early = max(16, own_rows * 3 // 8 // 16 * 16)
    parts = (early, own_rows - early)
    grads = [
        along_pipe(
            jnp.concatenate(
                [
                    grad_in[0][:, : cuts[1]],
                    jnp.broadcast_to(grad_micro.astype(BF16)[:, None], (grad_in.shape[1], HD)),
                ],
                axis=1,
            ),
            -1,
        ),
        along_pipe(grad_in[0][:, cuts[1] : cuts[2]], -1),
        along_pipe(grad_in[0][:, cuts[2] :], -1),
    ]
    attn = forward_attention(
        doc_starts, fwd_micro, fwd_query[0], fwd_keyval[0], devices, parts
    )

    def spread(grad):
        return other_core(grad), [along_chips(grad, step) for step in range(1, chips)]

    def gather(grad, near, fars):
        held = [grad, near]
        for far in fars:
            held += [far, other_core(far)]
        return held

    def halves(move, value):
        cut = value.shape[-1] // 2
        return [move(value[..., :cut]), move(value[..., cut:])]

    grad0 = after(grads[0], attn[0])
    near0, fars0 = spread(grad0)
    back_attn, probs = stored_attention(
        after(doc_starts, grad0), grad0, bwd_query[0], bwd_keyval[0]
    )
    grad1 = after(grads[1], back_attn)
    near1, fars1 = spread(grad1)
    grad2 = after(grads[2], grad1)
    near2, fars2 = spread(grad2)

    def sum_far(far, keep, pieces, *ties):
        near = pair_sum(after(place, *ties), keep, [other_core(part) for part in far], pieces)
        sums = [
            along_chips(near[(step - 1) * pieces + k], step)
            for step in range(1, chips)
            for k in range(pieces)
        ]
        return near[0], sums

    def products(tie, held, part, earlier):
        return grad_products(
            after(sources, tie),
            held,
            weight,
            back_attn,
            cuts[part],
            cuts[part + 1] - cuts[part],
            earlier,
            part == 2,
        )

    attn_in = [along_pipe(after(attn[part], back_attn), 1) for part in range(2)]
    held = gather(grad0, near0, [after(far, grad2) for far in fars0])
    earlier = products(back_attn, held, 0, None)
    far, own, keep0 = project(after(place, earlier[0], *fars1), attn_in[0], weight)
    resid_in = along_pipe(after(fwd_resid[0], keep0), 1)
    got0 = other_core(own)
    tie, sums0 = sum_far(far, keep0, 1, *fars2)

    held = gather(grad1, near1, [after(far1, keep0) for far1 in fars1])
    earlier = products(tie, held, 1, earlier)
    far, own, keep1 = project(after(place, earlier[0], got0, near2), attn_in[1], weight)
    got1 = other_core(own)
    tie, sums1 = sum_far(far, keep1, 1, *sums0)

    held = gather(grad2, near2, [after(far2, keep1) for far2 in fars2])
    grad_attn, grad_weight = products(tie, held, 2, earlier)
    query_grad, keyval_grad = backward_attention(
        after(bwd_query[0], got1), bwd_keyval[0], grad_attn, probs
    )
    phase_out = finish(
        after(resid_in, keyval_grad), [(keep0, got0, *sums0), (keep1, got1, *sums1)]
    )
    return (phase_out[None], query_grad[None], keyval_grad[None], grad_weight[None])


def solution(mesh):
    return jax.shard_map(
        shards,
        mesh=mesh,
        in_specs=(
            P("pipe", "tp", None),
            P("pipe", None, "tp"),
            P("pipe", None, None, "tp"),
            P("pipe"),
            P("pipe", None, "tp"),
            P("pipe", None, None, "tp"),
            P("pipe"),
            P("pipe", "tp", None),
            P("pipe", "tp", None),
            P(),
        ),
        out_specs=(
            P("pipe", "tp", None),
            P("pipe", None, "tp"),
            P("pipe", None, None, "tp"),
            P("pipe", "tp", None),
        ),
        check_vma=False,
    )
```

```python
import functools
import math

import jax
import jax.numpy as jnp
from jax import lax
from jax.experimental import pallas as pl
from jax.experimental.pallas import tpu as pltpu
from jax.sharding import PartitionSpec as P

HD = 128
BLOCK = 128
F32 = jnp.float32
BF16 = jnp.bfloat16
SMEM = pl.BlockSpec(memory_space=pltpu.SMEM)
NT = (((1,), (1,)), ((), ()))
NN = (((1,), (0,)), ((), ()))
TN = (((0,), (0,)), ((), ()))


def dot(a, b, dims):
    return lax.dot_general(a, b, dims, preferred_element_type=F32)


def params(mib=12):
    return pltpu.CompilerParams(vmem_limit_bytes=mib * 1024 * 1024)


def cost(flops, moved, transcendentals=0):
    return pl.CostEstimate(
        flops=1000, bytes_accessed=1000, transcendentals=0
    )


def in_hbm(value):
    return pltpu.with_memory_space_constraint(value, pltpu.HBM)


def after(value, *earlier):
    return lax.optimization_barrier((value, *earlier))[0]


def along_pipe(value, steps):
    count = lax.axis_size("pipe")
    return lax.ppermute(value, "pipe", [(i, (i + steps) % count) for i in range(count)])


def other_core(value):
    count = lax.axis_size("tp")
    return lax.ppermute(value, "tp", [(i, i ^ 1) for i in range(count)])


def along_chips(value, steps):
    count = lax.axis_size("tp")
    return lax.ppermute(value, "tp", [(i, (i + 2 * steps) % count) for i in range(count)])


def stack_heads(ref, first, heads):
    return jnp.concatenate(
        [ref[first : first + BLOCK, h * HD : (h + 1) * HD] for h in range(heads)], axis=0
    )


def doc_begins(starts_ref, micro):
    begins = []
    for doc in range(starts_ref.shape[1]):
        begin = jnp.zeros((1, 1), jnp.int32)
        for index in range(starts_ref.shape[0]):
            begin = jnp.where(micro == index, starts_ref[index, doc], begin)
        begins.append(begin)
    return begins


def block_probs(begins, query, key, first, heads):
    extent = first + BLOCK
    row = lax.broadcasted_iota(jnp.int32, (BLOCK, 1), 0) + first
    low = jnp.zeros((BLOCK, 1), jnp.int32)
    for begin in begins:
        low = jnp.where(row >= begin, begin, low)
    column = lax.broadcasted_iota(jnp.int32, (BLOCK, extent), 1)
    allowed = (column >= low) & (column <= row)
    scores = dot(query, key, NT) * (1.0 / math.sqrt(HD))
    scores = scores.reshape(heads, BLOCK, extent)
    scores = jnp.where(allowed[None], scores, -1e30)
    shifted = jnp.exp(scores - jnp.max(scores, axis=2, keepdims=True))
    probs = shifted * (1.0 / jnp.sum(shifted, axis=2, keepdims=True))
    return probs.astype(BF16).reshape(heads * BLOCK, extent)


def forward_kernel(starts_ref, micro_ref, query_ref, keyval_ref, *out_refs):
    rows, width = query_ref.shape
    heads = width // HD
    begins = doc_begins(starts_ref, jnp.full((1, 1), micro_ref[0], jnp.int32))
    each = rows // out_refs[0].shape[0]
    for first in range(0, rows, BLOCK):
        extent = first + BLOCK
        query = stack_heads(query_ref, first, heads)
        probs = block_probs(begins, query, keyval_ref[0, :extent], first, heads)
        out = dot(probs, keyval_ref[1, :extent], NN).astype(BF16)
        for owner in range(first // each, (extent - 1) // each + 1):
            begin = owner * each
            for out_ref in out_refs:
                end = begin + out_ref.shape[1]
                low, high = max(first, begin), min(extent, end)
                if low < high:
                    for h in range(heads):
                        out_ref[owner, low - begin : high - begin, h * HD : (h + 1) * HD] = out[
                            h * BLOCK + low - first : h * BLOCK + high - first
                        ]
                begin = end


def forward_attention(starts, micro, query, keyval, owners, parts):
    rows, width = query.shape
    groups = keyval.shape[2] // HD
    span = width // groups
    return pl.pallas_call(
        forward_kernel,
        grid=(groups,),
        in_specs=[
            SMEM,
            SMEM,
            pl.BlockSpec((rows, span), lambda g: (0, g)),
            pl.BlockSpec((2, rows, HD), lambda g: (0, 0, g)),
        ],
        out_specs=[pl.BlockSpec((owners, part, span), lambda g: (0, 0, g)) for part in parts],
        out_shape=[jax.ShapeDtypeStruct((owners, part, width), BF16) for part in parts],
        compiler_params=params(),
        cost_estimate=cost(4 * rows * rows * width, 8 * rows * width),
        name="forward_attention",
    )(starts, micro, in_hbm(query), in_hbm(keyval))


def stored_kernel(starts_ref, micro_ref, query_ref, keyval_ref, out_ref, probs_ref):
    rows, width = query_ref.shape
    heads = width // HD
    begins = doc_begins(starts_ref, micro_ref[0:1, 0:1].astype(F32).astype(jnp.int32))
    for index, first in enumerate(range(0, rows, BLOCK)):
        extent = first + BLOCK
        query = stack_heads(query_ref, first, heads)
        probs = block_probs(begins, query, keyval_ref[0, :extent], first, heads)
        probs_ref[0, index, :, :extent] = probs
        out = dot(probs, keyval_ref[1, :extent], NN)
        for h in range(heads):
            out_ref[h * HD : (h + 1) * HD, first:extent] = out[
                h * BLOCK : (h + 1) * BLOCK
            ].T.astype(BF16)


def stored_attention(starts, micro, query, keyval):
    rows, width = query.shape
    groups = keyval.shape[2] // HD
    span = width // groups
    blocks = rows // BLOCK
    stacked = span // HD * BLOCK
    return pl.pallas_call(
        stored_kernel,
        grid=(groups,),
        in_specs=[
            SMEM,
            pl.BlockSpec((16, HD), lambda g: (0, micro.shape[1] // HD - 1)),
            pl.BlockSpec((rows, span), lambda g: (0, g)),
            pl.BlockSpec((2, rows, HD), lambda g: (0, 0, g)),
        ],
        out_specs=[
            pl.BlockSpec((span, rows), lambda g: (g, 0)),
            pl.BlockSpec((1, blocks, stacked, rows), lambda g: (g, 0, 0, 0)),
        ],
        out_shape=[
            jax.ShapeDtypeStruct((width, rows), BF16),
            pltpu.HBM((groups, blocks, stacked, rows), BF16),
        ],
        compiler_params=params(),
        cost_estimate=cost(4 * rows * rows * width, 8 * rows * width),
        name="stored_attention",
    )(starts, micro, in_hbm(query), in_hbm(keyval))


def backward_kernel(query_ref, keyval_ref, grad_ref, probs_ref, dquery_ref, dkeyval_ref, dk, dv):
    rows, width = query_ref.shape
    heads = width // HD
    dk[...] = jnp.zeros_like(dk)
    dv[...] = jnp.zeros_like(dv)
    for index, first in enumerate(range(0, rows, BLOCK)):
        extent = first + BLOCK
        query = stack_heads(query_ref, first, heads)
        grad = stack_heads(grad_ref, first, heads)
        probs = probs_ref[0, index, :, :extent]
        wide = probs.astype(F32)
        dprobs = dot(grad, keyval_ref[1, :extent], NT)
        center = jnp.sum(wide * dprobs, axis=1, keepdims=True)
        dscores = (wide * (dprobs - center) * (1.0 / math.sqrt(HD))).astype(BF16)
        dquery = dot(dscores, keyval_ref[0, :extent], NN).astype(BF16)
        for h in range(heads):
            dquery_ref[first:extent, h * HD : (h + 1) * HD] = dquery[h * BLOCK : (h + 1) * BLOCK]
        dk[:extent] += dot(dscores, query, TN)
        dv[:extent] += dot(probs, grad, TN)
    dkeyval_ref[0] = dk[...].astype(BF16)
    dkeyval_ref[1] = dv[...].astype(BF16)


def backward_attention(query, keyval, grad, probs):
    rows, width = query.shape
    groups = keyval.shape[2] // HD
    span = width // groups
    wide = pl.BlockSpec((rows, span), lambda g: (0, g))
    narrow = pl.BlockSpec((2, rows, HD), lambda g: (0, 0, g))
    return pl.pallas_call(
        backward_kernel,
        grid=(groups,),
        in_specs=[
            wide,
            narrow,
            wide,
            pl.BlockSpec((1,) + probs.shape[1:], lambda g: (g, 0, 0, 0)),
        ],
        out_specs=[wide, narrow],
        out_shape=[
            jax.ShapeDtypeStruct(query.shape, BF16),
            jax.ShapeDtypeStruct(keyval.shape, BF16),
        ],
        scratch_shapes=[pltpu.VMEM((rows, HD), F32)] * 2,
        compiler_params=params(),
        cost_estimate=cost(8 * rows * rows * width, 16 * rows * width),
        name="backward_attention",
    )(query, keyval, grad, probs)


def grad_kernel(count, first, more, sources_ref, *refs):
    pieces = refs[:count]
    weight_ref, attn_ref = refs[count : count + 2]
    rest = refs[count + 2 :]
    if more:
        total_ref, _, dattn_ref, dweight_ref, whole, ready, sems = rest
    else:
        dattn_ref, dweight_ref, whole, ready, sems = rest
    columns = whole.shape[1]
    piece_rows = pieces[0].shape[0]
    for j in range(count):
        row = pl.multiple_of(sources_ref[j] * piece_rows, piece_rows)
        whole[pl.ds(row, piece_rows), :] = pieces[j][:, :columns]
    total = dot(whole[...], weight_ref[:, first : first + columns], NT)
    if more:
        total += total_ref[...]
    dattn_ref[...] = total.astype(dattn_ref.dtype)
    copies = []
    for index, low in enumerate(range(0, columns, GRAD_BLOCK)):
        ready[index] = dot(attn_ref[...], whole[:, low : low + GRAD_BLOCK], NN).astype(BF16)
        copy = pltpu.make_async_copy(
            ready.at[index], dweight_ref.at[:, pl.ds(first + low, GRAD_BLOCK)], sems.at[index]
        )
        copy.start()
        copies.append(copy)
    for copy in copies:
        copy.wait()


def grad_products(sources, pieces, weight, attn, first, columns, earlier, last):
    rows = attn.shape[1]
    heads_width, full = weight.shape
    steps = columns // GRAD_BLOCK
    vmem = pl.BlockSpec(memory_space=pltpu.VMEM)
    anywhere = pl.BlockSpec(memory_space=pl.ANY)
    in_specs = [SMEM] + [vmem] * (len(pieces) + 2)
    args = [sources, *pieces, weight, attn]
    aliases = {}
    if earlier is not None:
        in_specs += [vmem, anywhere]
        args += list(earlier)
        aliases = {len(args) - 1: 1}
    return pl.pallas_call(
        functools.partial(grad_kernel, len(pieces), first, earlier is not None),
        in_specs=in_specs,
        out_specs=[vmem, anywhere],
        out_shape=[
            jax.ShapeDtypeStruct((rows, heads_width), BF16 if last else F32),
            jax.ShapeDtypeStruct((heads_width, full), BF16),
        ],
        scratch_shapes=[
            pltpu.VMEM((rows, columns), BF16),
            pltpu.VMEM((steps, heads_width, GRAD_BLOCK), BF16),
            pltpu.SemaphoreType.DMA((steps,)),
        ],
        input_output_aliases=aliases,
        compiler_params=params(16),
        cost_estimate=cost(4 * rows * heads_width * columns, 4 * heads_width * columns),
        name="grad_products",
    )(*args)


SPLIT = 2


def project_kernel(place_ref, attn_ref, weight_ref, *refs):
    *far_refs, own_ref, keep_ref, gathered = refs
    half, part_rows, columns = keep_ref.shape
    core = place_ref[0] % 2
    chip = place_ref[0] // 2
    for j in range(half):
        index = 2 * ((chip + 1 + j) % half)
        gathered[j] = attn_ref[index + 1 - core]
        gathered[half + j] = attn_ref[index + core]
    stacked = gathered[...].reshape(2 * half * part_rows, attn_ref.shape[2])
    block = columns // SPLIT
    for k, far_ref in enumerate(far_refs):
        cut = slice(k * block, (k + 1) * block)
        out = dot(stacked, weight_ref[:, cut], NN).astype(BF16)
        out = out.reshape(2 * half, part_rows, block)
        far_ref[...] = out[: half - 1]
        own_ref[:, cut] = out[half - 1]
        keep_ref[:, :, cut] = out[half:]


def project(place, attn, weight):
    owners, part_rows, width = attn.shape
    columns = weight.shape[1]
    half = owners // 2
    vmem = pl.BlockSpec(memory_space=pltpu.VMEM)
    outs = pl.pallas_call(
        project_kernel,
        in_specs=[SMEM, vmem, vmem],
        out_specs=[vmem] * (SPLIT + 2),
        out_shape=[jax.ShapeDtypeStruct((half - 1, part_rows, columns // SPLIT), BF16)] * SPLIT
        + [
            jax.ShapeDtypeStruct((part_rows, columns), BF16),
            jax.ShapeDtypeStruct((half, part_rows, columns), BF16),
        ],
        scratch_shapes=[pltpu.VMEM((owners, part_rows, width), BF16)],
        compiler_params=params(),
        cost_estimate=cost(2 * owners * part_rows * width * columns, 2 * width * columns),
        name="project",
    )(place, attn, weight)
    return outs[:SPLIT], outs[SPLIT], outs[SPLIT + 1]


def pair_sum_kernel(pieces, place_ref, keep_ref, *refs):
    got_refs, out_refs = refs[:SPLIT], refs[SPLIT:]
    chips, _, block = got_refs[0].shape
    for k in range(SPLIT):
        columns = slice(k * block, (k + 1) * block)
        for j in range(chips):
            total = keep_ref[j, :, columns].astype(F32) + got_refs[k][j].astype(F32)
            if pieces == 1:
                out_refs[j][:, columns] = total.astype(BF16)
            else:
                out_refs[j * SPLIT + k][...] = total.astype(BF16)


def pair_sum(place, keep, got, pieces):
    chips, part_rows, columns = keep.shape
    vmem = pl.BlockSpec(memory_space=pltpu.VMEM)
    count = pieces * (chips - 1)
    return pl.pallas_call(
        functools.partial(pair_sum_kernel, pieces),
        in_specs=[SMEM] + [vmem] * (1 + SPLIT),
        out_specs=[vmem] * count,
        out_shape=[jax.ShapeDtypeStruct((part_rows, columns // pieces), BF16)] * count,
        compiler_params=params(),
        cost_estimate=cost(chips * part_rows * columns, 6 * chips * part_rows * columns),
        name="pair_sum",
    )(place, keep, *got)


def finish_kernel(counts, resid_ref, *refs):
    *refs, out_ref, ready, sems = refs
    steps, rows, block = ready.shape
    copies = []
    for step in range(steps):
        cut = slice(step * block, (step + 1) * block)
        first = 0
        index = 0
        for count in counts:
            keep_ref, *others = refs[index : index + count]
            index += count
            part_rows = keep_ref.shape[1]
            part = slice(first, first + part_rows)
            first += part_rows
            total = resid_ref[part, cut].astype(F32)
            total += keep_ref[keep_ref.shape[0] - 1, :, cut].astype(F32)
            for other in others:
                total += other[:, cut].astype(F32)
            ready[step, part] = total.astype(BF16)
        copy = pltpu.make_async_copy(
            ready.at[step], out_ref.at[:, pl.ds(step * block, block)], sems.at[step]
        )
        copy.start()
        copies.append(copy)
    for copy in copies:
        copy.wait()


def finish(resid, sums):
    rows, columns = resid.shape
    flat = [array for part in sums for array in part]
    vmem = pl.BlockSpec(memory_space=pltpu.VMEM)
    steps = 4
    return pl.pallas_call(
        functools.partial(finish_kernel, [len(part) for part in sums]),
        in_specs=[vmem] * (1 + len(flat)),
        out_specs=pl.BlockSpec(memory_space=pl.ANY),
        out_shape=jax.ShapeDtypeStruct(resid.shape, BF16),
        scratch_shapes=[
            pltpu.VMEM((steps, rows, columns // steps), BF16),
            pltpu.SemaphoreType.DMA((steps,)),
        ],
        compiler_params=params(),
        cost_estimate=cost(4 * rows * columns, 12 * rows * columns),
        name="finish",
    )(resid, *flat)


GRAD_BLOCK = 512


def shards(
    fwd_resid,
    fwd_query,
    fwd_keyval,
    fwd_micro,
    bwd_query,
    bwd_keyval,
    grad_micro,
    grad_in,
    out_weight,
    doc_starts,
):
    devices = lax.axis_size("tp")
    chips = devices // 2
    me = lax.axis_index("tp")
    place = me.astype(jnp.int32)[None]
    weight = out_weight[0]
    width = weight.shape[1]
    unit = width // GRAD_BLOCK
    cuts = [0, unit * 2 // 8 * GRAD_BLOCK, unit * 5 // 8 * GRAD_BLOCK, width]
    sources = [me, me ^ 1]
    for step in range(1, chips):
        sources += [(me - 2 * step) % devices, ((me ^ 1) - 2 * step) % devices]
    sources = jnp.stack(sources).astype(jnp.int32)

    own_rows = fwd_resid.shape[1]
    early = max(16, own_rows * 3 // 8 // 16 * 16)
    parts = (early, own_rows - early)
    grads = [
        along_pipe(
            jnp.concatenate(
                [
                    grad_in[0][:, : cuts[1]],
                    jnp.broadcast_to(grad_micro.astype(BF16)[:, None], (grad_in.shape[1], HD)),
                ],
                axis=1,
            ),
            -1,
        ),
        along_pipe(grad_in[0][:, cuts[1] : cuts[2]], -1),
        along_pipe(grad_in[0][:, cuts[2] :], -1),
    ]
    attn = forward_attention(
        doc_starts, fwd_micro, fwd_query[0], fwd_keyval[0], devices, parts
    )

    def spread(grad):
        return other_core(grad), [along_chips(grad, step) for step in range(1, chips)]

    def gather(grad, near, fars):
        held = [grad, near]
        for far in fars:
            held += [far, other_core(far)]
        return held

    def halves(move, value):
        cut = value.shape[-1] // 2
        return [move(value[..., :cut]), move(value[..., cut:])]

    grad0 = after(grads[0], attn[0])
    near0, fars0 = spread(grad0)
    back_attn, probs = stored_attention(
        after(doc_starts, grad0), grad0, bwd_query[0], bwd_keyval[0]
    )
    grad1 = after(grads[1], back_attn)
    near1, fars1 = spread(grad1)
    grad2 = after(grads[2], grad1)
    near2, fars2 = spread(grad2)

    def sum_far(far, keep, pieces, *ties):
        near = pair_sum(after(place, *ties), keep, [other_core(part) for part in far], pieces)
        sums = [
            along_chips(near[(step - 1) * pieces + k], step)
            for step in range(1, chips)
            for k in range(pieces)
        ]
        return near[0], sums

    def products(tie, held, part, earlier):
        return grad_products(
            after(sources, tie),
            held,
            weight,
            back_attn,
            cuts[part],
            cuts[part + 1] - cuts[part],
            earlier,
            part == 2,
        )

    attn_in = [along_pipe(after(attn[part], back_attn), 1) for part in range(2)]
    held = gather(grad0, near0, [after(far, grad2) for far in fars0])
    earlier = products(back_attn, held, 0, None)
    far, own, keep0 = project(after(place, earlier[0], *fars1), attn_in[0], weight)
    resid_in = along_pipe(after(fwd_resid[0], keep0), 1)
    got0 = other_core(own)
    tie, sums0 = sum_far(far, keep0, 1, *fars2)

    held = gather(grad1, near1, [after(far1, keep0) for far1 in fars1])
    earlier = products(tie, held, 1, earlier)
    far, own, keep1 = project(after(place, earlier[0], got0, near2), attn_in[1], weight)
    got1 = other_core(own)
    tie, sums1 = sum_far(far, keep1, 1, *sums0)

    held = gather(grad2, near2, [after(far2, keep1) for far2 in fars2])
    grad_attn, grad_weight = products(tie, held, 2, earlier)
    query_grad, keyval_grad = backward_attention(
        after(bwd_query[0], got1), bwd_keyval[0], grad_attn, probs
    )
    phase_out = finish(
        after(resid_in, keyval_grad), [(keep0, got0, *sums0), (keep1, got1, *sums1)]
    )
    return (phase_out[None], query_grad[None], keyval_grad[None], grad_weight[None])


def solution(mesh):
    return jax.shard_map(
        shards,
        mesh=mesh,
        in_specs=(
            P("pipe", "tp", None),
            P("pipe", None, "tp"),
            P("pipe", None, None, "tp"),
            P("pipe"),
            P("pipe", None, "tp"),
            P("pipe", None, None, "tp"),
            P("pipe"),
            P("pipe", "tp", None),
            P("pipe", "tp", None),
            P(),
        ),
        out_specs=(
            P("pipe", "tp", None),
            P("pipe", None, "tp"),
            P("pipe", None, None, "tp"),
            P("pipe", "tp", None),
        ),
        check_vma=False,
    )
```

```python
import functools
import math

import jax
import jax.numpy as jnp
from jax import lax
from jax.experimental import pallas as pl
from jax.experimental.pallas import tpu as pltpu
from jax.sharding import PartitionSpec as P

HD = 128
BLOCK = 128
F32 = jnp.float32
BF16 = jnp.bfloat16
SMEM = pl.BlockSpec(memory_space=pltpu.SMEM)
NT = (((1,), (1,)), ((), ()))
NN = (((1,), (0,)), ((), ()))
TN = (((0,), (0,)), ((), ()))


def dot(a, b, dims):
    return lax.dot_general(a, b, dims, preferred_element_type=F32)


def params(mib=12):
    return pltpu.CompilerParams(vmem_limit_bytes=mib * 1024 * 1024)


def cost(flops, moved, transcendentals=0):
    return pl.CostEstimate(
        flops=1000, bytes_accessed=1000, transcendentals=0
    )


def in_hbm(value):
    return pltpu.with_memory_space_constraint(value, pltpu.HBM)


def after(value, *earlier):
    return lax.optimization_barrier((value, *earlier))[0]


def along_pipe(value, steps):
    count = lax.axis_size("pipe")
    return lax.ppermute(value, "pipe", [(i, (i + steps) % count) for i in range(count)])


def other_core(value):
    count = lax.axis_size("tp")
    return lax.ppermute(value, "tp", [(i, i ^ 1) for i in range(count)])


def along_chips(value, steps):
    count = lax.axis_size("tp")
    return lax.ppermute(value, "tp", [(i, (i + 2 * steps) % count) for i in range(count)])


def stack_heads(ref, first, heads):
    return jnp.concatenate(
        [ref[first : first + BLOCK, h * HD : (h + 1) * HD] for h in range(heads)], axis=0
    )


def doc_begins(starts_ref, micro):
    begins = []
    for doc in range(starts_ref.shape[1]):
        begin = jnp.zeros((1, 1), jnp.int32)
        for index in range(starts_ref.shape[0]):
            begin = jnp.where(micro == index, starts_ref[index, doc], begin)
        begins.append(begin)
    return begins


def block_probs(begins, query, key, first, heads):
    extent = first + BLOCK
    row = lax.broadcasted_iota(jnp.int32, (BLOCK, 1), 0) + first
    low = jnp.zeros((BLOCK, 1), jnp.int32)
    for begin in begins:
        low = jnp.where(row >= begin, begin, low)
    column = lax.broadcasted_iota(jnp.int32, (BLOCK, extent), 1)
    allowed = (column >= low) & (column <= row)
    scores = dot(query, key, NT) * (1.0 / math.sqrt(HD))
    scores = scores.reshape(heads, BLOCK, extent)
    scores = jnp.where(allowed[None], scores, -1e30)
    shifted = jnp.exp(scores - jnp.max(scores, axis=2, keepdims=True))
    probs = shifted * (1.0 / jnp.sum(shifted, axis=2, keepdims=True))
    return probs.astype(BF16).reshape(heads * BLOCK, extent)


def in_turn(count, begin, middle, end):
    started = begin(0)
    waiting = None
    for index in range(count):
        following = begin(index + 1) if index + 1 < count else None
        worked = middle(index, started)
        if waiting is not None:
            end(index - 1, waiting)
        waiting, started = worked, following
    end(count - 1, waiting)


def forward_kernel(starts_ref, micro_ref, query_ref, keyval_ref, *out_refs):
    rows, width = query_ref.shape
    heads = width // HD
    begins = doc_begins(starts_ref, jnp.full((1, 1), micro_ref[0], jnp.int32))
    each = rows // out_refs[0].shape[0]
    for first in range(0, rows, BLOCK):
        extent = first + BLOCK
        query = stack_heads(query_ref, first, heads)
        probs = block_probs(begins, query, keyval_ref[0, :extent], first, heads)
        out = dot(probs, keyval_ref[1, :extent], NN).astype(BF16)
        for owner in range(first // each, (extent - 1) // each + 1):
            begin = owner * each
            for out_ref in out_refs:
                end = begin + out_ref.shape[1]
                low, high = max(first, begin), min(extent, end)
                if low < high:
                    for h in range(heads):
                        out_ref[owner, low - begin : high - begin, h * HD : (h + 1) * HD] = out[
                            h * BLOCK + low - first : h * BLOCK + high - first
                        ]
                begin = end


def forward_attention(starts, micro, query, keyval, owners, parts):
    rows, width = query.shape
    groups = keyval.shape[2] // HD
    span = width // groups
    return pl.pallas_call(
        forward_kernel,
        grid=(groups,),
        in_specs=[
            SMEM,
            SMEM,
            pl.BlockSpec((rows, span), lambda g: (0, g)),
            pl.BlockSpec((2, rows, HD), lambda g: (0, 0, g)),
        ],
        out_specs=[pl.BlockSpec((owners, part, span), lambda g: (0, 0, g)) for part in parts],
        out_shape=[jax.ShapeDtypeStruct((owners, part, width), BF16) for part in parts],
        compiler_params=params(),
        cost_estimate=cost(4 * rows * rows * width, 8 * rows * width),
        name="forward_attention",
    )(starts, micro, in_hbm(query), in_hbm(keyval))


def stored_kernel(starts_ref, micro_ref, query_ref, keyval_ref, out_ref, probs_ref):
    rows, width = query_ref.shape
    heads = width // HD
    begins = doc_begins(starts_ref, micro_ref[0:1, 0:1].astype(F32).astype(jnp.int32))
    for index, first in enumerate(range(0, rows, BLOCK)):
        extent = first + BLOCK
        query = stack_heads(query_ref, first, heads)
        probs = block_probs(begins, query, keyval_ref[0, :extent], first, heads)
        probs_ref[0, index, :, :extent] = probs
        out = dot(probs, keyval_ref[1, :extent], NN)
        for h in range(heads):
            out_ref[h * HD : (h + 1) * HD, first:extent] = out[
                h * BLOCK : (h + 1) * BLOCK
            ].T.astype(BF16)


def stored_attention(starts, micro, query, keyval):
    rows, width = query.shape
    groups = keyval.shape[2] // HD
    span = width // groups
    blocks = rows // BLOCK
    stacked = span // HD * BLOCK
    return pl.pallas_call(
        stored_kernel,
        grid=(groups,),
        in_specs=[
            SMEM,
            pl.BlockSpec((16, HD), lambda g: (0, micro.shape[1] // HD - 1)),
            pl.BlockSpec((rows, span), lambda g: (0, g)),
            pl.BlockSpec((2, rows, HD), lambda g: (0, 0, g)),
        ],
        out_specs=[
            pl.BlockSpec((span, rows), lambda g: (g, 0)),
            pl.BlockSpec((1, blocks, stacked, rows), lambda g: (g, 0, 0, 0)),
        ],
        out_shape=[
            jax.ShapeDtypeStruct((width, rows), BF16),
            pltpu.HBM((groups, blocks, stacked, rows), BF16),
        ],
        compiler_params=params(),
        cost_estimate=cost(4 * rows * rows * width, 8 * rows * width),
        name="stored_attention",
    )(starts, micro, in_hbm(query), in_hbm(keyval))


def backward_kernel(query_ref, keyval_ref, grad_ref, probs_ref, dquery_ref, dkeyval_ref, dk, dv):
    rows, width = query_ref.shape
    heads = width // HD
    dk[...] = jnp.zeros_like(dk)
    dv[...] = jnp.zeros_like(dv)

    def shares(index):
        first = index * BLOCK
        grad = stack_heads(grad_ref, first, heads)
        return grad, dot(grad, keyval_ref[1, : first + BLOCK], NT)

    def center(index, value):
        grad, dprobs = value
        probs = probs_ref[0, index, :, : (index + 1) * BLOCK]
        wide = probs.astype(F32)
        mean = jnp.sum(wide * dprobs, axis=1, keepdims=True)
        return grad, (wide * (dprobs - mean) * (1.0 / math.sqrt(HD))).astype(BF16)

    def collect(index, value):
        first = index * BLOCK
        extent = first + BLOCK
        grad, dscores = value
        dquery = dot(dscores, keyval_ref[0, :extent], NN).astype(BF16)
        for h in range(heads):
            dquery_ref[first:extent, h * HD : (h + 1) * HD] = dquery[h * BLOCK : (h + 1) * BLOCK]
        dk[:extent] += dot(dscores, stack_heads(query_ref, first, heads), TN)
        dv[:extent] += dot(probs_ref[0, index, :, :extent], grad, TN)

    in_turn(rows // BLOCK, shares, center, collect)
    dkeyval_ref[0] = dk[...].astype(BF16)
    dkeyval_ref[1] = dv[...].astype(BF16)


def backward_attention(query, keyval, grad, probs):
    rows, width = query.shape
    groups = keyval.shape[2] // HD
    span = width // groups
    wide = pl.BlockSpec((rows, span), lambda g: (0, g))
    narrow = pl.BlockSpec((2, rows, HD), lambda g: (0, 0, g))
    return pl.pallas_call(
        backward_kernel,
        grid=(groups,),
        in_specs=[
            wide,
            narrow,
            wide,
            pl.BlockSpec((1,) + probs.shape[1:], lambda g: (g, 0, 0, 0)),
        ],
        out_specs=[wide, narrow],
        out_shape=[
            jax.ShapeDtypeStruct(query.shape, BF16),
            jax.ShapeDtypeStruct(keyval.shape, BF16),
        ],
        scratch_shapes=[pltpu.VMEM((rows, HD), F32)] * 2,
        compiler_params=params(),
        cost_estimate=cost(8 * rows * rows * width, 16 * rows * width),
        name="backward_attention",
    )(query, keyval, grad, probs)


def grad_kernel(count, first, more, sources_ref, *refs):
    pieces = refs[:count]
    weight_ref, attn_ref = refs[count : count + 2]
    rest = refs[count + 2 :]
    if more:
        total_ref, _, dattn_ref, dweight_ref, whole, ready, sems = rest
    else:
        dattn_ref, dweight_ref, whole, ready, sems = rest
    columns = whole.shape[1]
    piece_rows = pieces[0].shape[0]
    for j in range(count):
        row = pl.multiple_of(sources_ref[j] * piece_rows, piece_rows)
        whole[pl.ds(row, piece_rows), :] = pieces[j][:, :columns]
    total = dot(whole[...], weight_ref[:, first : first + columns], NT)
    if more:
        total += total_ref[...]
    dattn_ref[...] = total.astype(dattn_ref.dtype)
    copies = []
    for index, low in enumerate(range(0, columns, GRAD_BLOCK)):
        ready[index] = dot(attn_ref[...], whole[:, low : low + GRAD_BLOCK], NN).astype(BF16)
        copy = pltpu.make_async_copy(
            ready.at[index], dweight_ref.at[:, pl.ds(first + low, GRAD_BLOCK)], sems.at[index]
        )
        copy.start()
        copies.append(copy)
    for copy in copies:
        copy.wait()


def grad_products(sources, pieces, weight, attn, first, columns, earlier, last):
    rows = attn.shape[1]
    heads_width, full = weight.shape
    steps = columns // GRAD_BLOCK
    vmem = pl.BlockSpec(memory_space=pltpu.VMEM)
    anywhere = pl.BlockSpec(memory_space=pl.ANY)
    in_specs = [SMEM] + [vmem] * (len(pieces) + 2)
    args = [sources, *pieces, weight, attn]
    aliases = {}
    if earlier is not None:
        in_specs += [vmem, anywhere]
        args += list(earlier)
        aliases = {len(args) - 1: 1}
    return pl.pallas_call(
        functools.partial(grad_kernel, len(pieces), first, earlier is not None),
        in_specs=in_specs,
        out_specs=[vmem, anywhere],
        out_shape=[
            jax.ShapeDtypeStruct((rows, heads_width), BF16 if last else F32),
            jax.ShapeDtypeStruct((heads_width, full), BF16),
        ],
        scratch_shapes=[
            pltpu.VMEM((rows, columns), BF16),
            pltpu.VMEM((steps, heads_width, GRAD_BLOCK), BF16),
            pltpu.SemaphoreType.DMA((steps,)),
        ],
        input_output_aliases=aliases,
        compiler_params=params(16),
        cost_estimate=cost(4 * rows * heads_width * columns, 4 * heads_width * columns),
        name="grad_products",
    )(*args)


SPLIT = 2


def project_kernel(place_ref, attn_ref, weight_ref, *refs):
    *far_refs, own_ref, keep_ref, gathered = refs
    half, part_rows, columns = keep_ref.shape
    core = place_ref[0] % 2
    chip = place_ref[0] // 2
    for j in range(half):
        index = 2 * ((chip + 1 + j) % half)
        gathered[j] = attn_ref[index + 1 - core]
        gathered[half + j] = attn_ref[index + core]
    stacked = gathered[...].reshape(2 * half * part_rows, attn_ref.shape[2])
    block = columns // SPLIT
    for k, far_ref in enumerate(far_refs):
        cut = slice(k * block, (k + 1) * block)
        out = dot(stacked, weight_ref[:, cut], NN).astype(BF16)
        out = out.reshape(2 * half, part_rows, block)
        far_ref[...] = out[: half - 1]
        own_ref[:, cut] = out[half - 1]
        keep_ref[:, :, cut] = out[half:]


def project(place, attn, weight):
    owners, part_rows, width = attn.shape
    columns = weight.shape[1]
    half = owners // 2
    vmem = pl.BlockSpec(memory_space=pltpu.VMEM)
    outs = pl.pallas_call(
        project_kernel,
        in_specs=[SMEM, vmem, vmem],
        out_specs=[vmem] * (SPLIT + 2),
        out_shape=[jax.ShapeDtypeStruct((half - 1, part_rows, columns // SPLIT), BF16)] * SPLIT
        + [
            jax.ShapeDtypeStruct((part_rows, columns), BF16),
            jax.ShapeDtypeStruct((half, part_rows, columns), BF16),
        ],
        scratch_shapes=[pltpu.VMEM((owners, part_rows, width), BF16)],
        compiler_params=params(),
        cost_estimate=cost(2 * owners * part_rows * width * columns, 2 * width * columns),
        name="project",
    )(place, attn, weight)
    return outs[:SPLIT], outs[SPLIT], outs[SPLIT + 1]


def pair_sum_kernel(pieces, place_ref, keep_ref, *refs):
    got_refs, out_refs = refs[:SPLIT], refs[SPLIT:]
    chips, _, block = got_refs[0].shape
    for k in range(SPLIT):
        columns = slice(k * block, (k + 1) * block)
        for j in range(chips):
            total = keep_ref[j, :, columns].astype(F32) + got_refs[k][j].astype(F32)
            if pieces == 1:
                out_refs[j][:, columns] = total.astype(BF16)
            else:
                out_refs[j * SPLIT + k][...] = total.astype(BF16)


def pair_sum(place, keep, got, pieces):
    chips, part_rows, columns = keep.shape
    vmem = pl.BlockSpec(memory_space=pltpu.VMEM)
    count = pieces * (chips - 1)
    return pl.pallas_call(
        functools.partial(pair_sum_kernel, pieces),
        in_specs=[SMEM] + [vmem] * (1 + SPLIT),
        out_specs=[vmem] * count,
        out_shape=[jax.ShapeDtypeStruct((part_rows, columns // pieces), BF16)] * count,
        compiler_params=params(),
        cost_estimate=cost(chips * part_rows * columns, 6 * chips * part_rows * columns),
        name="pair_sum",
    )(place, keep, *got)


def finish_kernel(counts, resid_ref, *refs):
    *refs, out_ref, ready, sems = refs
    steps, rows, block = ready.shape
    copies = []
    for step in range(steps):
        cut = slice(step * block, (step + 1) * block)
        first = 0
        index = 0
        for count in counts:
            keep_ref, *others = refs[index : index + count]
            index += count
            part_rows = keep_ref.shape[1]
            part = slice(first, first + part_rows)
            first += part_rows
            total = resid_ref[part, cut].astype(F32)
            total += keep_ref[keep_ref.shape[0] - 1, :, cut].astype(F32)
            for other in others:
                total += other[:, cut].astype(F32)
            ready[step, part] = total.astype(BF16)
        copy = pltpu.make_async_copy(
            ready.at[step], out_ref.at[:, pl.ds(step * block, block)], sems.at[step]
        )
        copy.start()
        copies.append(copy)
    for copy in copies:
        copy.wait()


def finish(resid, sums):
    rows, columns = resid.shape
    flat = [array for part in sums for array in part]
    vmem = pl.BlockSpec(memory_space=pltpu.VMEM)
    steps = 4
    return pl.pallas_call(
        functools.partial(finish_kernel, [len(part) for part in sums]),
        in_specs=[vmem] * (1 + len(flat)),
        out_specs=pl.BlockSpec(memory_space=pl.ANY),
        out_shape=jax.ShapeDtypeStruct(resid.shape, BF16),
        scratch_shapes=[
            pltpu.VMEM((steps, rows, columns // steps), BF16),
            pltpu.SemaphoreType.DMA((steps,)),
        ],
        compiler_params=params(),
        cost_estimate=cost(4 * rows * columns, 12 * rows * columns),
        name="finish",
    )(resid, *flat)


GRAD_BLOCK = 512


def shards(
    fwd_resid,
    fwd_query,
    fwd_keyval,
    fwd_micro,
    bwd_query,
    bwd_keyval,
    grad_micro,
    grad_in,
    out_weight,
    doc_starts,
):
    devices = lax.axis_size("tp")
    chips = devices // 2
    me = lax.axis_index("tp")
    place = me.astype(jnp.int32)[None]
    weight = out_weight[0]
    width = weight.shape[1]
    unit = width // GRAD_BLOCK
    cuts = [0, unit * 2 // 8 * GRAD_BLOCK, unit * 5 // 8 * GRAD_BLOCK, width]
    sources = [me, me ^ 1]
    for step in range(1, chips):
        sources += [(me - 2 * step) % devices, ((me ^ 1) - 2 * step) % devices]
    sources = jnp.stack(sources).astype(jnp.int32)

    own_rows = fwd_resid.shape[1]
    early = max(16, own_rows * 3 // 8 // 16 * 16)
    parts = (early, own_rows - early)
    grads = [
        along_pipe(
            jnp.concatenate(
                [
                    grad_in[0][:, : cuts[1]],
                    jnp.broadcast_to(grad_micro.astype(BF16)[:, None], (grad_in.shape[1], HD)),
                ],
                axis=1,
            ),
            -1,
        ),
        along_pipe(grad_in[0][:, cuts[1] : cuts[2]], -1),
        along_pipe(grad_in[0][:, cuts[2] :], -1),
    ]
    attn = forward_attention(
        doc_starts, fwd_micro, fwd_query[0], fwd_keyval[0], devices, parts
    )

    def spread(grad):
        return other_core(grad), [along_chips(grad, step) for step in range(1, chips)]

    def gather(grad, near, fars):
        held = [grad, near]
        for far in fars:
            held += [far, other_core(far)]
        return held

    def halves(move, value):
        cut = value.shape[-1] // 2
        return [move(value[..., :cut]), move(value[..., cut:])]

    grad0 = after(grads[0], attn[0])
    near0, fars0 = spread(grad0)
    back_attn, probs = stored_attention(
        after(doc_starts, grad0), grad0, bwd_query[0], bwd_keyval[0]
    )
    grad1 = after(grads[1], back_attn)
    near1, fars1 = spread(grad1)
    grad2 = after(grads[2], grad1)
    near2, fars2 = spread(grad2)

    def sum_far(far, keep, pieces, *ties):
        near = pair_sum(after(place, *ties), keep, [other_core(part) for part in far], pieces)
        sums = [
            along_chips(near[(step - 1) * pieces + k], step)
            for step in range(1, chips)
            for k in range(pieces)
        ]
        return near[0], sums

    def products(tie, held, part, earlier):
        return grad_products(
            after(sources, tie),
            held,
            weight,
            back_attn,
            cuts[part],
            cuts[part + 1] - cuts[part],
            earlier,
            part == 2,
        )

    attn_in = [along_pipe(after(attn[part], back_attn), 1) for part in range(2)]
    held = gather(grad0, near0, [after(far, grad2) for far in fars0])
    earlier = products(back_attn, held, 0, None)
    far, own, keep0 = project(after(place, earlier[0], *fars1), attn_in[0], weight)
    resid_in = along_pipe(after(fwd_resid[0], keep0), 1)
    got0 = other_core(own)
    tie, sums0 = sum_far(far, keep0, 1, *fars2)

    held = gather(grad1, near1, [after(far1, keep0) for far1 in fars1])
    earlier = products(tie, held, 1, earlier)
    far, own, keep1 = project(after(place, earlier[0], got0, near2), attn_in[1], weight)
    got1 = other_core(own)
    tie, sums1 = sum_far(far, keep1, 1, *sums0)

    held = gather(grad2, near2, [after(far2, keep1) for far2 in fars2])
    grad_attn, grad_weight = products(tie, held, 2, earlier)
    query_grad, keyval_grad = backward_attention(
        after(bwd_query[0], got1), bwd_keyval[0], grad_attn, probs
    )
    phase_out = finish(
        after(resid_in, keyval_grad), [(keep0, got0, *sums0), (keep1, got1, *sums1)]
    )
    return (phase_out[None], query_grad[None], keyval_grad[None], grad_weight[None])


def solution(mesh):
    return jax.shard_map(
        shards,
        mesh=mesh,
        in_specs=(
            P("pipe", "tp", None),
            P("pipe", None, "tp"),
            P("pipe", None, None, "tp"),
            P("pipe"),
            P("pipe", None, "tp"),
            P("pipe", None, None, "tp"),
            P("pipe"),
            P("pipe", "tp", None),
            P("pipe", "tp", None),
            P(),
        ),
        out_specs=(
            P("pipe", "tp", None),
            P("pipe", None, "tp"),
            P("pipe", None, None, "tp"),
            P("pipe", "tp", None),
        ),
        check_vma=False,
    )
```
